512 devices in a mesh: gz: 32 (over z_lo, x, core), gy: 16 (over z_hi, y).
Axes of the slice: x: 4, y: 4, z: 16 (z_hi: 4, z_lo: 4; z = z_hi * 4 + z_lo), core: 2. Of those that a mesh axis runs over, the one named last changes fastest.
Arguments:
- current: float32 [2, 256, 512, 512], P(None, 'gz', 'gy'), may hold values from -6 to 6
- kernel: float32 [2, 256, 512, 512], P(None, 'gz', 'gy'), may hold values from -6 to 6
Outputs:
- potential: float32 [2, 256, 512, 512], P(None, 'gz', 'gy')
The draws below stay inside these ranges and needn't reach their ends.
All inputs are finite; a program needn't handle non-finite values.
Results may differ from the reference program's by a relative error of at most 0.00007.
Values sent between devices are 32-bit elements; how exact they have to be, the bound alone decides.
A program may use at most 64 MiB of HBM per device.

```python
import jax
import jax.numpy as jnp
from jax import lax

NX = 512
NY = 512
NZ = 256


def levels(own_key, dims, shards, smallest, high):
    def one(position, parts):
        heights = jax.random.uniform(jax.random.fold_in(jax.random.fold_in(own_key, 6), position), (parts,), jnp.float32, smallest / len(shards), high / len(shards))
        return jnp.repeat(jnp.exp(heights), dims[position] // parts).reshape((-1,) + (1,) * (len(dims) - position - 1))

    loudness = one(*shards[0])
    for cut in shards[1:]:
        loudness = loudness * one(*cut)
    return loudness


def normal_values(rng, dims, scale, limit, split=(), dtype=jnp.bfloat16):
    values = jax.random.normal(rng, dims, jnp.float32) * scale
    if len(split) > 0:
        values = levels(rng, dims, split, -0.22, 0.18) * values
    return jnp.clip(values, min=-limit, max=limit).astype(dtype)


def setup_inputs(seed: int = 0) -> dict:
    splits = jax.random.split(jax.random.key(seed), 3)
    return {
        "current": normal_values(splits[0], (2, NZ, NY, NX), 1.0, 6.0, ((1, 32), (2, 16)), jnp.float32),
        "kernel": normal_values(splits[1], (2, NZ, NX, NY), 1.0, 6.0, ((1, 32), (2, 16)), jnp.float32),
    }


def one_plane(pair):
    src_plane, kern_plane = pair
    field = lax.complex(src_plane[0], src_plane[1])
    spectrum = jnp.fft.fft2(field)
    kern = lax.complex(kern_plane[0], kern_plane[1])
    product = spectrum * jnp.transpose(kern)
    result = jnp.fft.ifft2(product)
    return jnp.stack([jnp.real(result), jnp.imag(result)])


def reference(current, kernel):
    source = current - current[:, ::-1]
    planes_first = jnp.transpose(source, (1, 0, 2, 3))
    kernel_first = jnp.transpose(kernel, (1, 0, 2, 3))
    outcome = lax.map(one_plane, (planes_first, kernel_first))
    return jnp.transpose(outcome, (1, 0, 2, 3)).astype(jnp.float32)
```

```python
import functools

import jax
import jax.numpy as jnp
import ml_dtypes
import numpy as np
from jax import lax
from jax.experimental import pallas as pl
from jax.experimental.pallas import tpu as pltpu
from jax.sharding import PartitionSpec as P

MESH = pl.DeviceIdType.MESH
F32 = jnp.float32
BF16 = jnp.bfloat16


def two_terms(table):
    high = table.astype(ml_dtypes.bfloat16)
    low = (table - high.astype(np.float64)).astype(ml_dtypes.bfloat16)
    return np.stack([high, low])


def dft_tables(length, groups):
    index = np.arange(length)
    angle = (index[:, None] * index[None, :] % length) * (2.0 * np.pi / length)
    cos, sin = np.cos(angle), np.sin(angle)
    full = np.block([[cos, sin], [-sin, cos]])
    block = length // groups
    rows = full.reshape(2, groups, block, 2 * length).transpose(1, 0, 2, 3)
    rows = rows.reshape(2 * length, 2 * length)
    return two_terms(rows), two_terms(full.T)


def split(value):
    high = value.astype(BF16)
    return high, (value - high.astype(F32)).astype(BF16)


def dot_nt(a, b):
    return lax.dot_general(a, b, (((1,), (1,)), ((), ())), preferred_element_type=F32)


def dot_nn(a, b):
    return jnp.dot(a, b, preferred_element_type=F32)


def regroup(pieces):
    lane = lax.broadcasted_iota(jnp.int32, pieces[0].shape, 1)
    low = lane < 64
    even = lax.rem(lane // 32, 2) == 0
    v0, v1, v2, v3 = pieces

    def halves(a, b):
        return (
            jnp.where(low, a, pltpu.roll(b, 64, 1)),
            jnp.where(low, pltpu.roll(a, 64, 1), b),
        )

    def quarters(a, b):
        return (
            jnp.where(even, a, pltpu.roll(b, 32, 1)),
            jnp.where(even, pltpu.roll(a, 96, 1), b),
        )

    a0, a2 = halves(v0, v2)
    a1, a3 = halves(v1, v3)
    return quarters(a0, a1) + quarters(a2, a3)


def body(
    members,
    groups,
    scale,
    cur,
    kern,
    nt_hbm,
    nn_hbm,
    out,
    nt,
    nn,
    rhs,
    lhs1,
    lhs2,
    kmir,
    t1,
    r1,
    t2,
    r2,
    table_sem,
    k_send,
    k_recv,
    send1,
    recv1,
    send2,
    recv2,
):
    gz = lax.axis_index("gz")
    gy = lax.axis_index("gy")
    mirror = members - 1 - gz
    zh = gy // 4
    yc = lax.rem(gy, 4)

    load_nt = pltpu.make_async_copy(nt_hbm, nt, table_sem.at[0])
    load_nn = pltpu.make_async_copy(nn_hbm, nn, table_sem.at[1])
    load_nt.start()
    load_nn.start()

    def peer(side, dz, dy):
        other = lax.rem(zh + dz, 4) * 4 + lax.rem(yc + dy, 4)
        return gz + side * (mirror - gz), other

    barrier = pltpu.get_barrier_semaphore()

    def greet(e, carry):
        where = peer(e // 16, lax.rem(e // 4, 4), lax.rem(e, 4))
        pl.semaphore_signal(barrier, inc=1, device_id=where, device_id_type=MESH)
        return carry

    lax.fori_loop(1, 32, greet, 0)
    pl.semaphore_wait(barrier, 31)

    def kernel_copy(part):
        return pltpu.make_async_remote_copy(
            src_ref=kern.at[part, pl.ds(4, 4)],
            dst_ref=kmir.at[part],
            send_sem=k_send.at[part],
            recv_sem=k_recv.at[part],
            device_id=(mirror, gy),
            device_id_type=MESH,
        )

    kernel_copy(0).start()
    kernel_copy(1).start()

    def block_copy(t, r, send, recv, e):
        side = e // 16
        g, other = peer(side, lax.rem(e // 4, 4), lax.rem(e, 4))
        return pltpu.make_async_remote_copy(
            src_ref=t.at[side, other],
            dst_ref=r.at[side, gy],
            send_sem=send.at[e],
            recv_sem=recv.at[e],
            device_id=(g, other),
            device_id_type=MESH,
        )

    def transform_and_send(t, r, send, recv):
        def step(i, carry):
            dz = lax.rem(i + 1, 4)
            zb = lax.rem(zh + dz, 4)
            rows = pl.ds(pl.multiple_of(zb * 256, 256), 256)
            high, low = nt[0, rows, :], nt[1, rows, :]
            total = dot_nt(high, rhs[0]) + dot_nt(high, rhs[1]) + dot_nt(low, rhs[0])
            t[0, pl.ds(zb * 4, 4)] = total[:, :128].reshape(4, 64, 128)
            t[1, pl.ds(zb * 4, 4)] = total[:, 128:].reshape(4, 64, 128)

            def send_one(q, inner):
                e = (q // 4) * 16 + dz * 4 + lax.rem(q, 4)

                @pl.when(e > 0)
                def _():
                    block_copy(t, r, send, recv, e).start()

                return inner

            return lax.fori_loop(0, 8, send_one, carry)

        lax.fori_loop(0, 4, step, 0)
        r[0, gy] = t[0, gy]

    def receive_all(t, r, send, recv):
        def one(e, carry):
            block_copy(t, r, send, recv, e).wait_recv()
            return carry

        lax.fori_loop(1, 32, one, 0)

    def sent_all(t, r, send, recv):
        def one(e, carry):
            block_copy(t, r, send, recv, e).wait_send()
            return carry

        lax.fori_loop(1, 32, one, 0)

    for part in range(2):
        for place in range(8):
            plane = place if place < 4 else 11 - place
            high, low = split(cur[part, plane])
            rows, columns = pl.ds(place * 32, 32), pl.ds(part * 512, 512)
            rhs[0, rows, columns] = high
            rhs[1, rows, columns] = low
    load_nt.wait()
    transform_and_send(t1, r1, send1, recv1)
    load_nn.wait()
    receive_all(t1, r1, send1, recv1)

    def gather1(q, carry):
        rows = pl.ds(pl.multiple_of((q // 4) * 32, 32), 32)
        first = lax.rem(q, 4) * 4
        pieces = [r1[0, first + i, rows, :] - r1[1, first + i, rows, :] for i in range(4)]
        columns = pl.ds(pl.multiple_of(q * 128, 128), 128)
        for p, piece in enumerate(regroup(pieces)):
            high, low = split(piece)
            lhs1[p * 32 : p * 32 + 32, columns] = high
            lhs1[128 + p * 32 : 160 + p * 32, columns] = low
        return carry

    lax.fori_loop(0, 8, gather1, 0)
    kernel_copy(0).wait_recv()
    kernel_copy(1).wait_recv()

    def product(n, carry):
        def spectrum(part):
            columns = pl.ds(pl.multiple_of(part * 512 + n * 256, 256), 256)
            both = dot_nn(lhs1[...], nn[0, :, columns])
            return both[:128] + both[128:] + dot_nn(lhs1[:128], nn[1, :, columns])

        re, im = spectrum(0), spectrum(1)
        ky = pl.ds(pl.multiple_of(n * 256, 256), 256)
        ky_im = pl.ds(pl.multiple_of(512 + n * 256, 256), 256)

        def multiply(kre, kim, rows):
            high, low = split(re * kim + im * kre)
            rhs[0, rows, ky] = high
            rhs[1, rows, ky] = low
            high, low = split(re * kre - im * kim)
            rhs[0, rows, ky_im] = high
            rhs[1, rows, ky_im] = low

        multiply(
            kern[0, 0:4, :, ky].reshape(128, 256),
            kern[1, 0:4, :, ky].reshape(128, 256),
            pl.ds(0, 128),
        )
        multiply(
            -jnp.concatenate([kmir[0, 3 - p, :, ky] for p in range(4)], axis=0),
            -jnp.concatenate([kmir[1, 3 - p, :, ky] for p in range(4)], axis=0),
            pl.ds(128, 128),
        )
        return carry

    lax.fori_loop(0, 2, product, 0)

    transform_and_send(t2, r2, send2, recv2)
    receive_all(t2, r2, send2, recv2)

    def gather2(q, carry):
        rows = pl.ds(pl.multiple_of((q // 4) * 32, 32), 32)
        first = lax.rem(q, 4) * 4
        columns = pl.ds(pl.multiple_of(q * 128, 128), 128)
        for side in range(2):
            pieces = [r2[side, first + i, rows, :] for i in range(4)]
            for p, piece in enumerate(regroup(pieces)):
                plane = 7 - p if side else p
                high, low = split(piece)
                lhs2[plane * 32 : plane * 32 + 32, columns] = high
                lhs2[256 + plane * 32 : 288 + plane * 32, columns] = low
        return carry

    lax.fori_loop(0, 8, gather2, 0)

    def finish(n, carry):
        columns = pl.ds(pl.multiple_of(n * 256, 256), 256)
        both = dot_nn(lhs2[...], nn[0, :, columns])
        value = both[:256] + both[256:] + dot_nn(lhs2[:256], nn[1, :, columns])
        x = pl.ds(pl.multiple_of(lax.rem(n, 2) * 256, 256), 256)
        out[1 - n // 2, :, :, x] = (value * scale).reshape(8, 32, 256)
        return carry

    lax.fori_loop(0, 4, finish, 0)
    kernel_copy(0).wait_send()
    kernel_copy(1).wait_send()
    sent_all(t1, r1, send1, recv1)
    sent_all(t2, r2, send2, recv2)


def local(current, kernel):
    members = lax.axis_size("gz")
    groups = lax.axis_size("gy")
    nt, nn = dft_tables(512, groups)
    vmem = pl.BlockSpec(memory_space=pltpu.VMEM)
    anywhere = pl.BlockSpec(memory_space=pl.ANY)
    exchange = pltpu.VMEM((2, groups, 64, 128), F32)
    return pl.pallas_call(
        functools.partial(body, members, groups, 1.0 / (512 * 512)),
        out_shape=jax.ShapeDtypeStruct(current.shape, F32),
        in_specs=[vmem, vmem, anywhere, anywhere],
        out_specs=vmem,
        scratch_shapes=[
            pltpu.VMEM((2, 1024, 1024), BF16),
            pltpu.VMEM((2, 1024, 1024), BF16),
            pltpu.VMEM((2, 256, 1024), BF16),
            pltpu.VMEM((256, 1024), BF16),
            pltpu.VMEM((512, 1024), BF16),
            pltpu.VMEM((2, 4, 32, 512), F32),
            exchange,
            exchange,
            exchange,
            exchange,
            pltpu.SemaphoreType.DMA((2,)),
            pltpu.SemaphoreType.DMA((2,)),
            pltpu.SemaphoreType.DMA((2,)),
            pltpu.SemaphoreType.DMA((32,)),
            pltpu.SemaphoreType.DMA((32,)),
            pltpu.SemaphoreType.DMA((32,)),
            pltpu.SemaphoreType.DMA((32,)),
        ],
        compiler_params=pltpu.CompilerParams(
            collective_id=0, has_side_effects=True, vmem_limit_bytes=48 * 1024 * 1024
        ),
    )(current, kernel, jnp.asarray(nt), jnp.asarray(nn))


def solution(mesh):
    spec = P(None, "gz", "gy", None)
    return jax.shard_map(
        local, mesh=mesh, in_specs=(spec, spec), out_specs=spec, check_vma=False
    )
```

```python
import functools

import jax
import jax.numpy as jnp
import ml_dtypes
import numpy as np
from jax import lax
from jax.experimental import pallas as pl
from jax.experimental.pallas import tpu as pltpu
from jax.sharding import PartitionSpec as P

MESH = pl.DeviceIdType.MESH
F32 = jnp.float32
BF16 = jnp.bfloat16


def two_terms(table):
    high = table.astype(ml_dtypes.bfloat16)
    low = (table - high.astype(np.float64)).astype(ml_dtypes.bfloat16)
    return np.stack([high, low])


def dft_tables(length, groups):
    index = np.arange(length)
    angle = (index[:, None] * index[None, :] % length) * (2.0 * np.pi / length)
    cos, sin = np.cos(angle), np.sin(angle)
    full = np.block([[cos, sin], [-sin, cos]])
    block = length // groups
    rows = full.reshape(2, groups, block, 2 * length).transpose(1, 0, 2, 3)
    rows = rows.reshape(2 * length, 2 * length)
    return two_terms(rows), two_terms(full.T)


def split(value):
    high = value.astype(BF16)
    return high, (value - high.astype(F32)).astype(BF16)


def dot_nt(a, b):
    return lax.dot_general(a, b, (((1,), (1,)), ((), ())), preferred_element_type=F32)


def dot_nn(a, b):
    return jnp.dot(a, b, preferred_element_type=F32)


def regroup(pieces):
    lane = lax.broadcasted_iota(jnp.int32, pieces[0].shape, 1)
    low = lane < 64
    even = lax.rem(lane // 32, 2) == 0
    v0, v1, v2, v3 = pieces

    def halves(a, b):
        return (
            jnp.where(low, a, pltpu.roll(b, 64, 1)),
            jnp.where(low, pltpu.roll(a, 64, 1), b),
        )

    def quarters(a, b):
        return (
            jnp.where(even, a, pltpu.roll(b, 32, 1)),
            jnp.where(even, pltpu.roll(a, 96, 1), b),
        )

    a0, a2 = halves(v0, v2)
    a1, a3 = halves(v1, v3)
    return quarters(a0, a1) + quarters(a2, a3)


def body(
    members,
    scale,
    cur_hbm,
    kern_hbm,
    nt_hbm,
    nn_hbm,
    out,
    cur,
    kern,
    nt,
    nn,
    rhs,
    lhs,
    t1,
    met,
    diff,
    r1,
    t2,
    r2,
    load_sem,
    send1,
    recv1,
    send2,
    recv2,
    send3,
    recv3,
    send4,
    recv4,
):
    gz = lax.axis_index("gz")
    gy = lax.axis_index("gy")
    mirror = members - 1 - gz
    zh = gy // 4
    yc = lax.rem(gy, 4)
    side = gz // (members // 2)
    way = 1 - 2 * side
    sign = way.astype(F32)

    loads = [
        pltpu.make_async_copy(source, target, load_sem.at[i])
        for i, (source, target) in enumerate(
            [(cur_hbm, cur), (nt_hbm, nt), (nn_hbm, nn), (kern_hbm, kern)]
        )
    ]
    for load in loads:
        load.start()

    def column(dz):
        return lax.rem(zh + dz + 8, 4)

    def plane_at(place):
        return place + side * (7 - 2 * place)

    barrier = pltpu.get_barrier_semaphore()

    def greet(e, carry):
        other = column(lax.rem(e // 4, 4)) * 4 + lax.rem(yc + lax.rem(e, 4), 4)
        where = (gz + (e // 16) * (mirror - gz), other)
        pl.semaphore_signal(barrier, inc=1, device_id=where, device_id_type=MESH)
        return carry

    lax.fori_loop(1, 32, greet, 0)
    pl.semaphore_wait(barrier, 31)

    def rows_times_rhs(zb):
        rows = pl.ds(pl.multiple_of(zb * 256, 256), 256)
        high, low = nt[0, rows, :], nt[1, rows, :]
        return dot_nt(high, rhs[0]) + dot_nt(high, rhs[1]) + dot_nt(low, rhs[0])

    loads[0].wait()

    def take(place, carry):
        plane = plane_at(place)
        rows = pl.ds(pl.multiple_of(place * 32, 32), 32)
        for part in range(2):
            high, low = split(cur[part, plane])
            rhs[0, rows, part * 512 : part * 512 + 512] = high
            rhs[1, rows, part * 512 : part * 512 + 512] = low
        return carry

    lax.fori_loop(0, 8, take, 0)
    loads[1].wait()

    def forward_rows(dz):
        zb = column(dz)
        total = rows_times_rhs(zb)
        t1[0, pl.ds(zb * 4, 4)] = total[:, :128].reshape(4, 64, 128)
        t1[1, pl.ds(zb * 4, 4)] = total[:, 128:].reshape(4, 64, 128)

    def unit(k, by_side):
        along = way if by_side is side else -way
        return [(2, by_side), (along, 0), (along, 1), (0, by_side)][k]

    other_side = 1 - side

    def swap_copy(k):
        dz, half = unit(k, side)
        return pltpu.make_async_remote_copy(
            src_ref=t1.at[half, pl.ds(column(dz) * 4, 4)],
            dst_ref=met.at[k],
            send_sem=send1.at[k],
            recv_sem=recv1.at[k],
            device_id=(mirror, gy),
            device_id_type=MESH,
        )

    def subtract(k):
        dz, half = unit(k, other_side)
        diff[k] = (t1[half, pl.ds(column(dz) * 4, 4)] - met[k]) * sign

    def spread_copy(k, dy):
        dz, half = unit(k, other_side)
        yb = lax.rem(yc + dy, 4)
        target = gz if k == 3 else mirror
        return pltpu.make_async_remote_copy(
            src_ref=diff.at[k, yb],
            dst_ref=r1.at[half, gy],
            send_sem=send2.at[k * 4 + dy],
            recv_sem=recv2.at[k * 4 + dy],
            device_id=(target, column(dz) * 4 + yb),
            device_id_type=MESH,
        )

    def hand_copy(k):
        dz, half = unit(k, side)
        if k == 3:
            half = other_side
        rows = pl.ds(column(-dz) * 4, 4)
        return pltpu.make_async_remote_copy(
            src_ref=r1.at[half, rows],
            dst_ref=r1.at[half, rows],
            send_sem=send3.at[k],
            recv_sem=recv3.at[k],
            device_id=(mirror, gy),
            device_id_type=MESH,
        )

    def meet(k):
        swap_copy(k).wait_recv()
        subtract(k)

        def start(dy, carry):
            spread_copy(k, dy).start()
            return carry

        if k == 3:
            r1[other_side, gy] = diff[3, yc]
        lax.fori_loop(1 if k == 3 else 0, 4, start, 0)

    def hand(k):
        def wait(dy, carry):
            spread_copy(k, dy).wait_recv()
            return carry

        lax.fori_loop(1 if k == 3 else 0, 4, wait, 0)
        hand_copy(k).start()

    forward_rows(2)
    swap_copy(0).start()
    forward_rows(way)
    swap_copy(1).start()
    forward_rows(0)
    forward_rows(-way)
    swap_copy(2).start()
    meet(0)
    swap_copy(3).start()
    meet(1)
    hand(0)
    meet(2)
    hand(1)
    meet(3)
    hand(2)
    hand(3)
    loads[2].wait()
    loads[3].wait()
    for k in range(4):
        hand_copy(k).wait_recv()

    def gather(read, row_of):
        def one(q, carry):
            rows = pl.ds(pl.multiple_of((q // 4) * 32, 32), 32)
            first = lax.rem(q, 4) * 4
            columns = pl.ds(pl.multiple_of(q * 128, 128), 128)
            for half in range(2):
                pieces = [read(half, first + i, rows) for i in range(4)]
                for p, piece in enumerate(regroup(pieces)):
                    high, low = split(piece)
                    start = row_of(half * 4 + p) * 32
                    lhs[0, pl.ds(pl.multiple_of(start, 32), 32), columns] = high
                    lhs[1, pl.ds(pl.multiple_of(start, 32), 32), columns] = low
            return carry

        lax.fori_loop(0, 8, one, 0)

    def lhs_times(columns):
        both = dot_nn(lhs[...].reshape(512, 1024), nn[0, :, columns])
        return both[:256] + both[256:] + dot_nn(lhs[0], nn[1, :, columns])

    gather(lambda half, s, rows: r1[half, s, rows, :], lambda place: place)

    def product(n, carry):
        ky = pl.ds(pl.multiple_of(n * 256, 256), 256)
        ky_im = pl.ds(pl.multiple_of(512 + n * 256, 256), 256)
        re, im = lhs_times(ky), lhs_times(ky_im)
        kre = jnp.concatenate([kern[0, plane_at(p), :, ky] for p in range(8)], axis=0)
        kim = jnp.concatenate([kern[1, plane_at(p), :, ky] for p in range(8)], axis=0)
        high, low = split(re * kim + im * kre)
        rhs[0, :, ky] = high
        rhs[1, :, ky] = low
        high, low = split(re * kre - im * kim)
        rhs[0, :, ky_im] = high
        rhs[1, :, ky_im] = low
        return carry

    lax.fori_loop(0, 2, product, 0)

    def return_copy(e):
        other = column(e // 4) * 4 + lax.rem(yc + e, 4)
        return pltpu.make_async_remote_copy(
            src_ref=t2.at[other],
            dst_ref=r2.at[gy],
            send_sem=send4.at[e],
            recv_sem=recv4.at[e],
            device_id=(gz, other),
            device_id_type=MESH,
        )

    def inverse_rows(i, carry):
        dz = lax.rem(2 + 3 * i + 3 * (i * (i + 3) // 2 - 2 * i), 4)
        zb = column(dz)
        t2[pl.ds(zb * 4, 4)] = rows_times_rhs(zb).reshape(4, 64, 256)

        def start(dy, inner):
            e = dz * 4 + dy

            @pl.when(e > 0)
            def _():
                return_copy(e).start()

            return inner

        return lax.fori_loop(0, 4, start, carry)

    lax.fori_loop(0, 4, inverse_rows, 0)
    r2[gy] = t2[gy]

    def arrived(e, carry):
        return_copy(e).wait_recv()
        return carry

    lax.fori_loop(1, 16, arrived, 0)

    def read_back(half, s, rows):
        return r2[s, rows, half * 128 : half * 128 + 128]

    gather(read_back, plane_at)
    factor = sign * scale

    def finish(n, carry):
        columns = pl.ds(pl.multiple_of(n * 256, 256), 256)
        x = pl.ds(pl.multiple_of(lax.rem(n, 2) * 256, 256), 256)
        out[1 - n // 2, :, :, x] = (lhs_times(columns) * factor).reshape(8, 32, 256)
        return carry

    lax.fori_loop(0, 4, finish, 0)

    def sent(e, carry):
        return_copy(e).wait_send()
        return carry

    lax.fori_loop(1, 16, sent, 0)
    for k in range(4):
        swap_copy(k).wait_send()
        hand_copy(k).wait_send()
        for dy in range(1 if k == 3 else 0, 4):
            spread_copy(k, dy).wait_send()


def local(current, kernel):
    members = lax.axis_size("gz")
    groups = lax.axis_size("gy")
    nt, nn = dft_tables(512, groups)
    anywhere = pl.BlockSpec(memory_space=pl.ANY)
    table = pltpu.VMEM((2, 1024, 1024), BF16)
    operand = pltpu.VMEM((2, 256, 1024), BF16)
    block = pltpu.VMEM(current.shape, F32)
    halves = pltpu.VMEM((2, groups, 64, 128), F32)
    units = pltpu.VMEM((4, 4, 64, 128), F32)
    whole = pltpu.VMEM((groups, 64, 256), F32)
    dma = pltpu.SemaphoreType.DMA
    return pl.pallas_call(
        functools.partial(body, members, 1.0 / (512 * 512)),
        out_shape=jax.ShapeDtypeStruct(current.shape, F32),
        in_specs=[anywhere] * 4,
        out_specs=pl.BlockSpec(memory_space=pltpu.VMEM),
        scratch_shapes=[block, block, table, table, operand, operand]
        + [halves, units, units, halves, whole, whole]
        + [dma((4,)), dma((4,)), dma((4,)), dma((16,)), dma((16,))]
        + [dma((4,)), dma((4,)), dma((16,)), dma((16,))],
        compiler_params=pltpu.CompilerParams(
            collective_id=0, has_side_effects=True, vmem_limit_bytes=56 * 1024 * 1024
        ),
    )(current, kernel, jnp.asarray(nt), jnp.asarray(nn))


def solution(mesh):
    spec = P(None, "gz", "gy", None)
    return jax.shard_map(
        local, mesh=mesh, in_specs=(spec, spec), out_specs=spec, check_vma=False
    )
```

```python
import functools

import jax
import jax.numpy as jnp
import ml_dtypes
import numpy as np
from jax import lax
from jax.experimental import pallas as pl
from jax.experimental.pallas import tpu as pltpu
from jax.sharding import PartitionSpec as P

MESH = pl.DeviceIdType.MESH
F32 = jnp.float32
BF16 = jnp.bfloat16


def two_terms(table):
    high = table.astype(ml_dtypes.bfloat16)
    low = (table - high.astype(np.float64)).astype(ml_dtypes.bfloat16)
    return np.stack([high, low])


def dft_tables(length, groups):
    index = np.arange(length)
    angle = (index[:, None] * index[None, :] % length) * (2.0 * np.pi / length)
    cos, sin = np.cos(angle), np.sin(angle)
    full = np.block([[cos, sin], [-sin, cos]])
    block = length // groups
    rows = full.reshape(2, groups, block, 2 * length).transpose(1, 0, 2, 3)
    rows = rows.reshape(2 * length, 2 * length)
    return two_terms(rows), two_terms(full.T)


def split(value):
    high = value.astype(BF16)
    return high, (value - high.astype(F32)).astype(BF16)


def dot_nt(a, b):
    return lax.dot_general(a, b, (((1,), (1,)), ((), ())), preferred_element_type=F32)


def dot_nn(a, b):
    return jnp.dot(a, b, preferred_element_type=F32)


def regroup(pieces):
    lane = lax.broadcasted_iota(jnp.int32, pieces[0].shape, 1)
    low = lane < 64
    even = lax.rem(lane // 32, 2) == 0
    v0, v1, v2, v3 = pieces

    def halves(a, b):
        return (
            jnp.where(low, a, pltpu.roll(b, 64, 1)),
            jnp.where(low, pltpu.roll(a, 64, 1), b),
        )

    def quarters(a, b):
        return (
            jnp.where(even, a, pltpu.roll(b, 32, 1)),
            jnp.where(even, pltpu.roll(a, 96, 1), b),
        )

    a0, a2 = halves(v0, v2)
    a1, a3 = halves(v1, v3)
    return quarters(a0, a1) + quarters(a2, a3)


def body(
    members,
    scale,
    cur_hbm,
    kern_hbm,
    nt_hbm,
    nn_hbm,
    out,
    cur,
    kern,
    nt,
    nn,
    rhs,
    lhs,
    t1,
    met,
    diff,
    r1,
    t2,
    r2,
    load_sem,
    send1,
    recv1,
    send2,
    recv2,
    send3,
    recv3,
    send4,
    recv4,
    relayed,
    send5,
    recv5,
):
    gz = lax.axis_index("gz")
    gy = lax.axis_index("gy")
    mirror = members - 1 - gz
    zh = gy // 4
    yc = lax.rem(gy, 4)
    side = gz // (members // 2)
    way = 1 - 2 * side
    sign = way.astype(F32)

    loads = [
        pltpu.make_async_copy(source, target, load_sem.at[i])
        for i, (source, target) in enumerate(
            [(cur_hbm, cur), (nt_hbm, nt), (nn_hbm, nn), (kern_hbm, kern)]
        )
    ]
    for load in loads:
        load.start()

    def column(dz):
        return lax.rem(zh + dz + 8, 4)

    def plane_at(place):
        return place + side * (7 - 2 * place)

    barrier = pltpu.get_barrier_semaphore()

    def greet(e, carry):
        other = column(lax.rem(e // 4, 4)) * 4 + lax.rem(yc + lax.rem(e, 4), 4)
        where = (gz + (e // 16) * (mirror - gz), other)
        pl.semaphore_signal(barrier, inc=1, device_id=where, device_id_type=MESH)
        return carry

    lax.fori_loop(1, 32, greet, 0)

    def rows_times_rhs(zb):
        rows = pl.ds(pl.multiple_of(zb * 256, 256), 256)
        high, low = nt[0, rows, :], nt[1, rows, :]
        return dot_nt(high, rhs[0]) + dot_nt(high, rhs[1]) + dot_nt(low, rhs[0])

    loads[0].wait()

    def take(place, carry):
        plane = plane_at(place)
        rows = pl.ds(pl.multiple_of(place * 32, 32), 32)
        for part in range(2):
            high, low = split(cur[part, plane])
            rhs[0, rows, part * 512 : part * 512 + 512] = high
            rhs[1, rows, part * 512 : part * 512 + 512] = low
        return carry

    lax.fori_loop(0, 8, take, 0)
    loads[1].wait()

    def forward_rows(dz):
        zb = column(dz)
        total = rows_times_rhs(zb)
        t1[0, pl.ds(zb * 4, 4)] = total[:, :128].reshape(4, 64, 128)
        t1[1, pl.ds(zb * 4, 4)] = total[:, 128:].reshape(4, 64, 128)

    def unit(k, by_side):
        along = way if by_side is side else -way
        return [(2, by_side), (along, 0), (along, 1), (0, by_side)][k]

    other_side = 1 - side

    def swap_copy(k):
        dz, half = unit(k, side)
        return pltpu.make_async_remote_copy(
            src_ref=t1.at[half, pl.ds(column(dz) * 4, 4)],
            dst_ref=met.at[k],
            send_sem=send1.at[k],
            recv_sem=recv1.at[k],
            device_id=(mirror, gy),
            device_id_type=MESH,
        )

    def subtract(k):
        dz, half = unit(k, other_side)
        diff[k] = (t1[half, pl.ds(column(dz) * 4, 4)] - met[k]) * sign

    def spread_copy(k, dy):
        dz, half = unit(k, other_side)
        yb = lax.rem(yc + dy, 4)
        target = gz if k == 3 else mirror
        return pltpu.make_async_remote_copy(
            src_ref=diff.at[k, yb],
            dst_ref=r1.at[half, gy],
            send_sem=send2.at[k * 4 + dy],
            recv_sem=recv2.at[k * 4 + dy],
            device_id=(target, column(dz) * 4 + yb),
            device_id_type=MESH,
        )

    def hand_copy(k):
        dz, half = unit(k, side)
        if k == 3:
            half = other_side
        rows = pl.ds(column(-dz) * 4, 4)
        return pltpu.make_async_remote_copy(
            src_ref=r1.at[half, rows],
            dst_ref=r1.at[half, rows],
            send_sem=send3.at[k],
            recv_sem=recv3.at[k],
            device_id=(mirror, gy),
            device_id_type=MESH,
        )

    def meet(k):
        swap_copy(k).wait_recv()
        subtract(k)

        def start(dy, carry):
            spread_copy(k, dy).start()
            return carry

        if k == 3:
            r1[other_side, gy] = diff[3, yc]
        lax.fori_loop(1 if k == 3 else 0, 4, start, 0)

    def hand(k):
        def wait(dy, carry):
            spread_copy(k, dy).wait_recv()
            return carry

        lax.fori_loop(1 if k == 3 else 0, 4, wait, 0)
        hand_copy(k).start()

    forward_rows(2)
    pl.semaphore_wait(barrier, 31)
    swap_copy(0).start()
    forward_rows(way)
    swap_copy(1).start()
    forward_rows(0)
    forward_rows(-way)
    swap_copy(2).start()
    meet(0)
    swap_copy(3).start()
    meet(1)
    hand(0)
    meet(2)
    hand(1)
    meet(3)
    hand(2)
    hand(3)
    loads[2].wait()
    loads[3].wait()
    for k in range(4):
        hand_copy(k).wait_recv()

    def gather(read, row_of):
        def one(q, carry):
            rows = pl.ds(pl.multiple_of((q // 4) * 32, 32), 32)
            first = lax.rem(q, 4) * 4
            columns = pl.ds(pl.multiple_of(q * 128, 128), 128)
            for half in range(2):
                pieces = [read(half, first + i, rows) for i in range(4)]
                for p, piece in enumerate(regroup(pieces)):
                    high, low = split(piece)
                    start = row_of(half * 4 + p) * 32
                    lhs[0, pl.ds(pl.multiple_of(start, 32), 32), columns] = high
                    lhs[1, pl.ds(pl.multiple_of(start, 32), 32), columns] = low
            return carry

        lax.fori_loop(0, 8, one, 0)

    def lhs_times(columns):
        both = dot_nn(lhs[...].reshape(512, 1024), nn[0, :, columns])
        return both[:256] + both[256:] + dot_nn(lhs[0], nn[1, :, columns])

    gather(lambda half, s, rows: r1[half, s, rows, :], lambda place: place)

    def product(n, carry):
        ky = pl.ds(pl.multiple_of(n * 256, 256), 256)
        ky_im = pl.ds(pl.multiple_of(512 + n * 256, 256), 256)
        re, im = lhs_times(ky), lhs_times(ky_im)
        kre = jnp.concatenate([kern[0, plane_at(p), :, ky] for p in range(8)], axis=0)
        kim = jnp.concatenate([kern[1, plane_at(p), :, ky] for p in range(8)], axis=0)
        high, low = split(re * kim + im * kre)
        rhs[0, :, ky] = high
        rhs[1, :, ky] = low
        high, low = split(re * kre - im * kim)
        rhs[0, :, ky_im] = high
        rhs[1, :, ky_im] = low
        return carry

    lax.fori_loop(0, 2, product, 0)

    def return_copy(e):
        other = column(e // 4) * 4 + lax.rem(yc + e, 4)
        return pltpu.make_async_remote_copy(
            src_ref=t2.at[other],
            dst_ref=r2.at[gy],
            send_sem=send4.at[e],
            recv_sem=recv4.at[e],
            device_id=(gz, other),
            device_id_type=MESH,
        )

    def up_or_down(dy):
        return 1 - 2 * (dy // 2)

    def first_leg(dy):
        yb = lax.rem(yc + dy, 4)
        return pltpu.make_async_remote_copy(
            src_ref=t2.at[column(2) * 4 + yb],
            dst_ref=relayed.at[dy],
            send_sem=send5.at[dy],
            recv_sem=recv5.at[dy],
            device_id=(gz, column(up_or_down(dy)) * 4 + yb),
            device_id_type=MESH,
        )

    def second_leg(dy):
        step = up_or_down(dy)
        origin = column(-step) * 4 + lax.rem(yc + 4 - dy, 4)
        return pltpu.make_async_remote_copy(
            src_ref=relayed.at[dy],
            dst_ref=r2.at[origin],
            send_sem=send4.at[8 + dy],
            recv_sem=recv4.at[8 + dy],
            device_id=(gz, column(step) * 4 + yc),
            device_id_type=MESH,
        )

    def inverse_rows(i, carry):
        dz = lax.rem(2 + 3 * i + 3 * (i * (i + 3) // 2 - 2 * i), 4)
        zb = column(dz)
        t2[pl.ds(zb * 4, 4)] = rows_times_rhs(zb).reshape(4, 64, 256)

        def start(dy, inner):
            e = dz * 4 + dy

            @pl.when((e > 0) & (dz != 2))
            def _():
                return_copy(e).start()

            @pl.when(dz == 2)
            def _():
                first_leg(dy).start()

            return inner

        return lax.fori_loop(0, 4, start, carry)

    lax.fori_loop(0, 4, inverse_rows, 0)
    r2[gy] = t2[gy]

    def relay(dy, carry):
        first_leg(dy).wait_recv()
        second_leg(dy).start()
        return carry

    lax.fori_loop(0, 4, relay, 0)

    def arrived(e, carry):
        return_copy(e).wait_recv()
        return carry

    def arrived_relayed(dy, carry):
        second_leg(dy).wait_recv()
        return carry

    lax.fori_loop(1, 8, arrived, 0)
    lax.fori_loop(12, 16, arrived, 0)
    lax.fori_loop(0, 4, arrived_relayed, 0)

    def read_back(half, s, rows):
        return r2[s, rows, half * 128 : half * 128 + 128]

    gather(read_back, plane_at)
    factor = sign * scale

    def finish(n, carry):
        columns = pl.ds(pl.multiple_of(n * 256, 256), 256)
        x = pl.ds(pl.multiple_of(lax.rem(n, 2) * 256, 256), 256)
        out[1 - n // 2, :, :, x] = (lhs_times(columns) * factor).reshape(8, 32, 256)
        return carry

    lax.fori_loop(0, 4, finish, 0)

    def sent(e, carry):
        return_copy(e).wait_send()
        return carry

    def sent_relayed(dy, carry):
        first_leg(dy).wait_send()
        second_leg(dy).wait_send()
        return carry

    lax.fori_loop(1, 8, sent, 0)
    lax.fori_loop(12, 16, sent, 0)
    lax.fori_loop(0, 4, sent_relayed, 0)
    for k in range(4):
        swap_copy(k).wait_send()
        hand_copy(k).wait_send()
        for dy in range(1 if k == 3 else 0, 4):
            spread_copy(k, dy).wait_send()


def local(current, kernel):
    members = lax.axis_size("gz")
    groups = lax.axis_size("gy")
    nt, nn = dft_tables(512, groups)
    anywhere = pl.BlockSpec(memory_space=pl.ANY)
    table = pltpu.VMEM((2, 1024, 1024), BF16)
    operand = pltpu.VMEM((2, 256, 1024), BF16)
    block = pltpu.VMEM(current.shape, F32)
    halves = pltpu.VMEM((2, groups, 64, 128), F32)
    units = pltpu.VMEM((4, 4, 64, 128), F32)
    whole = pltpu.VMEM((groups, 64, 256), F32)
    dma = pltpu.SemaphoreType.DMA
    return pl.pallas_call(
        functools.partial(body, members, 1.0 / (512 * 512)),
        out_shape=jax.ShapeDtypeStruct(current.shape, F32),
        in_specs=[anywhere] * 4,
        out_specs=pl.BlockSpec(memory_space=pltpu.VMEM),
        scratch_shapes=[block, block, table, table, operand, operand]
        + [halves, units, units, halves, whole, whole]
        + [dma((4,)), dma((4,)), dma((4,)), dma((16,)), dma((16,))]
        + [dma((4,)), dma((4,)), dma((16,)), dma((16,))]
        + [pltpu.VMEM((4, 64, 256), F32), dma((4,)), dma((4,))],
        compiler_params=pltpu.CompilerParams(
            collective_id=0, has_side_effects=True, vmem_limit_bytes=56 * 1024 * 1024
        ),
    )(current, kernel, jnp.asarray(nt), jnp.asarray(nn))


def solution(mesh):
    spec = P(None, "gz", "gy", None)
    return jax.shard_map(
        local, mesh=mesh, in_specs=(spec, spec), out_specs=spec, check_vma=False
    )
```

```python
import functools

import jax
import jax.numpy as jnp
import ml_dtypes
import numpy as np
from jax import lax
from jax.experimental import pallas as pl
from jax.experimental.pallas import tpu as pltpu
from jax.sharding import PartitionSpec as P

MESH = pl.DeviceIdType.MESH
F32 = jnp.float32
BF16 = jnp.bfloat16


def two_terms(table):
    high = table.astype(ml_dtypes.bfloat16)
    low = (table - high.astype(np.float64)).astype(ml_dtypes.bfloat16)
    return np.stack([high, low])


def dft_tables(length, groups):
    index = np.arange(length)
    angle = (index[:, None] * index[None, :] % length) * (2.0 * np.pi / length)
    cos, sin = np.cos(angle), np.sin(angle)
    full = np.block([[cos, sin], [-sin, cos]])
    half = length // groups // 2
    rows = full.reshape(2, groups, 2, half, 2 * length).transpose(1, 2, 0, 3, 4)
    rows = rows.reshape(2 * length, 2 * length)
    return two_terms(rows), two_terms(full.T)


def split(value):
    high = value.astype(BF16)
    return high, (value - high.astype(F32)).astype(BF16)


def dot_nt(a, b):
    return lax.dot_general(a, b, (((1,), (1,)), ((), ())), preferred_element_type=F32)


def dot_nn(a, b):
    return jnp.dot(a, b, preferred_element_type=F32)


def regroup(pieces):
    lane = lax.broadcasted_iota(jnp.int32, pieces[0].shape, 1)
    low = lane < 64
    even = lax.rem(lane // 32, 2) == 0
    v0, v1, v2, v3 = pieces

    def halves(a, b):
        return (
            jnp.where(low, a, pltpu.roll(b, 64, 1)),
            jnp.where(low, pltpu.roll(a, 64, 1), b),
        )

    def quarters(a, b):
        return (
            jnp.where(even, a, pltpu.roll(b, 32, 1)),
            jnp.where(even, pltpu.roll(a, 96, 1), b),
        )

    a0, a2 = halves(v0, v2)
    a1, a3 = halves(v1, v3)
    return quarters(a0, a1) + quarters(a2, a3)


def body(
    members,
    scale,
    cur_hbm,
    kern_hbm,
    nt_hbm,
    nn_hbm,
    out,
    cur,
    kern,
    nt,
    nn,
    rhs,
    back,
    lhs,
    t1,
    met,
    diff,
    r1,
    t2,
    r2,
    load_sem,
    send1,
    recv1,
    send2,
    recv2,
    send3,
    recv3,
    send4,
    recv4,
):
    gz = lax.axis_index("gz")
    gy = lax.axis_index("gy")
    mirror = members - 1 - gz
    zh = gy // 4
    yc = lax.rem(gy, 4)
    side = gz // (members // 2)
    other_side = 1 - side
    way = 1 - 2 * side
    sign = way.astype(F32)

    def column(dz):
        return lax.rem(zh + dz + 8, 4)

    def plane_at(place):
        return place + side * (7 - 2 * place)

    def table_rows(dz):
        return pl.ds(pl.multiple_of(column(dz) * 256, 256), 256)

    order = (2, way, 0, -way)
    load_cur = pltpu.make_async_copy(cur_hbm, cur, load_sem.at[0])
    load_kern = pltpu.make_async_copy(kern_hbm, kern, load_sem.at[1])
    load_nn = pltpu.make_async_copy(nn_hbm, nn, load_sem.at[2])
    load_nt = [
        pltpu.make_async_copy(
            nt_hbm.at[:, table_rows(dz)], nt.at[:, table_rows(dz)], load_sem.at[3 + i]
        )
        for i, dz in enumerate(order)
    ]
    load_cur.start()
    for load in load_nt:
        load.start()

    barrier = pltpu.get_barrier_semaphore()

    def greet(e, carry):
        other = column(lax.rem(e // 4, 4)) * 4 + lax.rem(yc + lax.rem(e, 4), 4)
        where = (gz + (e // 16) * (mirror - gz), other)
        pl.semaphore_signal(barrier, inc=1, device_id=where, device_id_type=MESH)
        return carry

    lax.fori_loop(1, 32, greet, 0)

    load_cur.wait()

    def take(place, carry):
        plane = plane_at(place)
        rows = pl.ds(pl.multiple_of(place * 32, 32), 32)
        for part in range(2):
            high, low = split(cur[part, plane])
            rhs[0, rows, part * 512 : part * 512 + 512] = high
            rhs[1, rows, part * 512 : part * 512 + 512] = low
        return carry

    lax.fori_loop(0, 8, take, 0)

    def forward_rows(i):
        load_nt[i].wait()
        high, low = nt[0, table_rows(order[i]), :], nt[1, table_rows(order[i]), :]
        total = dot_nt(high, rhs[0]) + dot_nt(high, rhs[1]) + dot_nt(low, rhs[0])
        targets = pl.ds(column(order[i]) * 4, 4)
        t1[0, targets] = total[:, :128].reshape(4, 64, 128)
        t1[1, targets] = total[:, 128:].reshape(4, 64, 128)

    slots = (pl.ds(64, 32), pl.ds(0, 64), pl.ds(96, 32))

    def half_rows(which):
        return pl.ds(pl.multiple_of(which * 32, 32), 32)

    def unit(u, which, along):
        rows = pl.ds(0, 64) if u == 1 else half_rows(which)
        return (2, along, 0)[u], rows

    def swap_copy(h, u):
        dz, rows = unit(u, side, way)
        return pltpu.make_async_remote_copy(
            src_ref=t1.at[h, pl.ds(column(dz) * 4, 4), rows],
            dst_ref=met.at[h, :, slots[u]],
            send_sem=send1.at[h * 3 + u],
            recv_sem=recv1.at[h * 3 + u],
            device_id=(mirror, gy),
            device_id_type=MESH,
        )

    def spread_copy(h, u, dy):
        dz, rows = unit(u, other_side, -way)
        yb = lax.rem(yc + dy, 4)
        target = gz if u == 2 else mirror
        return pltpu.make_async_remote_copy(
            src_ref=diff.at[h, yb, slots[u]],
            dst_ref=r1.at[h, gy, rows],
            send_sem=send2.at[h * 12 + u * 4 + dy],
            recv_sem=recv2.at[h * 12 + u * 4 + dy],
            device_id=(target, column(dz) * 4 + yb),
            device_id_type=MESH,
        )

    def hand_copy(h, u):
        dz, rows = unit(u, other_side if u == 2 else side, way)
        sources = pl.ds(column(-dz) * 4, 4)
        return pltpu.make_async_remote_copy(
            src_ref=r1.at[h, sources, rows],
            dst_ref=r1.at[h, sources, rows],
            send_sem=send3.at[h * 3 + u],
            recv_sem=recv3.at[h * 3 + u],
            device_id=(mirror, gy),
            device_id_type=MESH,
        )

    def meet(h, u):
        swap_copy(h, u).wait_recv()
        dz, rows = unit(u, other_side, -way)
        mine = t1[h, pl.ds(column(dz) * 4, 4), rows, :]
        diff[h, :, slots[u], :] = (mine - met[h, :, slots[u], :]) * sign

        def start(dy, carry):
            spread_copy(h, u, dy).start()
            return carry

        if u == 2:
            r1[h, gy, rows, :] = diff[h, yc, slots[u], :]
        lax.fori_loop(1 if u == 2 else 0, 4, start, 0)

    def hand(h, u):
        def wait(dy, carry):
            spread_copy(h, u, dy).wait_recv()
            return carry

        lax.fori_loop(1 if u == 2 else 0, 4, wait, 0)
        hand_copy(h, u).start()

    def gather(r, h, row_of):
        def one(q, carry):
            part = q // 4
            first = lax.rem(q, 4) * 4
            columns = pl.ds(pl.multiple_of(q * 128, 128), 128)
            upper = pl.ds(pl.multiple_of(part * 16, 16), 16)
            lower = pl.ds(pl.multiple_of(32 + part * 16, 16), 16)
            pieces = [
                jnp.concatenate([r[h, first + i, upper, :], r[h, first + i, lower, :]], axis=0)
                for i in range(4)
            ]
            for p, piece in enumerate(regroup(pieces)):
                high, low = split(piece)
                rows = pl.ds(pl.multiple_of(row_of(p) * 32, 32), 32)
                lhs[0, rows, columns] = high
                lhs[1, rows, columns] = low
            return carry

        lax.fori_loop(0, 8, one, 0)

    def lhs_times(columns):
        both = dot_nn(lhs[...].reshape(256, 1024), nn[0, :, columns])
        return both[:128] + both[128:] + dot_nn(lhs[0], nn[1, :, columns])

    def return_copy(h, e):
        other = column(e // 4) * 4 + lax.rem(yc + e, 4)
        return pltpu.make_async_remote_copy(
            src_ref=t2.at[h, other],
            dst_ref=r2.at[h, gy],
            send_sem=send4.at[h * 16 + e],
            recv_sem=recv4.at[h * 16 + e],
            device_id=(gz, other),
            device_id_type=MESH,
        )

    def middle(h):
        for u in range(3):
            hand_copy(h, u).wait_recv()

        gather(r1, h, lambda p: p)

        def product(n, carry):
            ky = pl.ds(pl.multiple_of(n * 256, 256), 256)
            ky_im = pl.ds(pl.multiple_of(512 + n * 256, 256), 256)
            re, im = lhs_times(ky), lhs_times(ky_im)
            planes = [plane_at(4 * h + p) for p in range(4)]
            kre = jnp.concatenate([kern[0, plane, :, ky] for plane in planes], axis=0)
            kim = jnp.concatenate([kern[1, plane, :, ky] for plane in planes], axis=0)
            high, low = split(re * kim + im * kre)
            back[0:128, ky] = high
            back[128:256, ky] = low
            high, low = split(re * kre - im * kim)
            back[0:128, ky_im] = high
            back[128:256, ky_im] = low
            return carry

        lax.fori_loop(0, 2, product, 0)

        def inverse_rows(i, carry):
            dz = lax.rem(2 + 3 * i + 3 * (i * (i + 3) // 2 - 2 * i), 4)
            both = dot_nt(nt[0, table_rows(dz), :], back[...])
            total = both[:, :128] + both[:, 128:]
            total += dot_nt(nt[1, table_rows(dz), :], back[0:128])
            t2[h, pl.ds(column(dz) * 4, 4)] = total.reshape(4, 64, 128)

            def start(dy, inner):
                e = dz * 4 + dy

                @pl.when(e > 0)
                def _():
                    return_copy(h, e).start()

                return inner

            return lax.fori_loop(0, 4, start, carry)

        lax.fori_loop(0, 4, inverse_rows, 0)
        r2[h, gy] = t2[h, gy]

    factor = sign * scale

    def finish(h):
        def arrived(e, carry):
            return_copy(h, e).wait_recv()
            return carry

        lax.fori_loop(1, 16, arrived, 0)
        gather(r2, h, lambda p: p)

        def columns_of(n, carry):
            columns = pl.ds(pl.multiple_of(n * 256, 256), 256)
            x = pl.ds(pl.multiple_of(lax.rem(n, 2) * 256, 256), 256)
            value = lhs_times(columns) * factor
            for p in range(4):
                out[1 - n // 2, plane_at(4 * h + p), :, x] = value[p * 32 : p * 32 + 32]
            return carry

        lax.fori_loop(0, 4, columns_of, 0)

    forward_rows(0)
    pl.semaphore_wait(barrier, 31)
    swap_copy(0, 0).start()
    load_nn.start()
    load_kern.start()
    forward_rows(1)
    swap_copy(0, 1).start()
    forward_rows(2)
    swap_copy(0, 2).start()
    forward_rows(3)
    meet(0, 0)
    swap_copy(1, 0).start()
    meet(0, 1)
    swap_copy(1, 1).start()
    hand(0, 0)
    meet(0, 2)
    swap_copy(1, 2).start()
    hand(0, 1)
    meet(1, 0)
    hand(0, 2)
    meet(1, 1)
    hand(1, 0)
    meet(1, 2)
    load_nn.wait()
    load_kern.wait()
    middle(0)
    hand(1, 1)
    hand(1, 2)
    middle(1)
    finish(0)
    finish(1)

    for h in range(2):
        for u in range(3):
            swap_copy(h, u).wait_send()
            hand_copy(h, u).wait_send()
            for dy in range(1 if u == 2 else 0, 4):
                spread_copy(h, u, dy).wait_send()

        def sent(e, carry):
            return_copy(h, e).wait_send()
            return carry

        lax.fori_loop(1, 16, sent, 0)


def local(current, kernel):
    members = lax.axis_size("gz")
    groups = lax.axis_size("gy")
    nt, nn = dft_tables(512, groups)
    anywhere = pl.BlockSpec(memory_space=pl.ANY)
    table = pltpu.VMEM((2, 1024, 1024), BF16)
    block = pltpu.VMEM(current.shape, F32)
    halves = pltpu.VMEM((2, groups, 64, 128), F32)
    units = pltpu.VMEM((2, 4, 128, 128), F32)
    dma = pltpu.SemaphoreType.DMA
    return pl.pallas_call(
        functools.partial(body, members, 1.0 / (512 * 512)),
        out_shape=jax.ShapeDtypeStruct(current.shape, F32),
        in_specs=[anywhere] * 4,
        out_specs=pl.BlockSpec(memory_space=pltpu.VMEM),
        scratch_shapes=[block, block, table, table]
        + [pltpu.VMEM((2, 256, 1024), BF16), pltpu.VMEM((256, 1024), BF16)]
        + [pltpu.VMEM((2, 128, 1024), BF16)]
        + [halves, units, units, halves, halves, halves]
        + [dma((7,)), dma((6,)), dma((6,)), dma((24,)), dma((24,))]
        + [dma((6,)), dma((6,)), dma((32,)), dma((32,))],
        compiler_params=pltpu.CompilerParams(
            collective_id=0, has_side_effects=True, vmem_limit_bytes=48 * 1024 * 1024
        ),
    )(current, kernel, jnp.asarray(nt), jnp.asarray(nn))


def solution(mesh):
    spec = P(None, "gz", "gy", None)
    return jax.shard_map(
        local, mesh=mesh, in_specs=(spec, spec), out_specs=spec, check_vma=False
    )
```

```python
import functools

import jax
import jax.numpy as jnp
import ml_dtypes
import numpy as np
from jax import lax
from jax.experimental import pallas as pl
from jax.experimental.pallas import tpu as pltpu
from jax.sharding import PartitionSpec as P

MESH = pl.DeviceIdType.MESH
F32 = jnp.float32
BF16 = jnp.bfloat16


def two_terms(table):
    high = table.astype(ml_dtypes.bfloat16)
    low = (table - high.astype(np.float64)).astype(ml_dtypes.bfloat16)
    return np.stack([high, low])


def dft_tables(length, groups):
    index = np.arange(length)
    angle = (index[:, None] * index[None, :] % length) * (2.0 * np.pi / length)
    cos, sin = np.cos(angle), np.sin(angle)
    full = np.block([[cos, sin], [-sin, cos]])
    block = length // groups
    rows = full.reshape(2, groups, block, 2 * length).transpose(1, 0, 2, 3)
    rows = rows.reshape(2 * length, 2 * length)
    down = full.T.reshape(2, 4, length // 4, 2 * length).transpose(1, 0, 2, 3)
    return two_terms(rows), two_terms(down.reshape(2 * length, 2 * length))


def split(value):
    high = value.astype(BF16)
    return high, (value - high.astype(F32)).astype(BF16)


def dot_nt(a, b):
    return lax.dot_general(a, b, (((1,), (1,)), ((), ())), preferred_element_type=F32)


def dot_nn(a, b):
    return jnp.dot(a, b, preferred_element_type=F32)


def regroup(pieces):
    lane = lax.broadcasted_iota(jnp.int32, pieces[0].shape, 1)
    low = lane < 64
    even = lax.rem(lane // 32, 2) == 0
    v0, v1, v2, v3 = pieces

    def halves(a, b):
        return (
            jnp.where(low, a, pltpu.roll(b, 64, 1)),
            jnp.where(low, pltpu.roll(a, 64, 1), b),
        )

    def quarters(a, b):
        return (
            jnp.where(even, a, pltpu.roll(b, 32, 1)),
            jnp.where(even, pltpu.roll(a, 96, 1), b),
        )

    a0, a2 = halves(v0, v2)
    a1, a3 = halves(v1, v3)
    return quarters(a0, a1) + quarters(a2, a3)


def body(
    members,
    scale,
    cur_hbm,
    kern_hbm,
    nt_hbm,
    nn_hbm,
    out,
    cur,
    kern,
    nt,
    nn,
    rhs,
    lhs,
    spectrum,
    t1,
    met,
    diff,
    r1,
    t2,
    r2,
    load_sem,
    send1,
    recv1,
    send2,
    recv2,
    send3,
    recv3,
    send4,
    recv4,
    relayed,
    send5,
    recv5,
):
    gz = lax.axis_index("gz")
    gy = lax.axis_index("gy")
    mirror = members - 1 - gz
    zh = gy // 4
    yc = lax.rem(gy, 4)
    side = gz // (members // 2)
    way = 1 - 2 * side
    sign = way.astype(F32)

    def column(dz):
        return lax.rem(zh + dz + 8, 4)

    def plane_at(place):
        return place + side * (7 - 2 * place)

    def table_rows(dz):
        return pl.ds(pl.multiple_of(column(dz) * 256, 256), 256)

    order = (2, way, 0, -way)
    load_cur = pltpu.make_async_copy(cur_hbm, cur, load_sem.at[0])
    load_kern = pltpu.make_async_copy(kern_hbm, kern, load_sem.at[1])
    load_nn = pltpu.make_async_copy(nn_hbm, nn, load_sem.at[2])
    load_nt = [
        pltpu.make_async_copy(
            nt_hbm.at[:, table_rows(dz)], nt.at[:, table_rows(dz)], load_sem.at[3 + i]
        )
        for i, dz in enumerate(order)
    ]
    load_cur.start()
    for load in load_nt:
        load.start()

    barrier = pltpu.get_barrier_semaphore()

    def greet(e, carry):
        other = column(lax.rem(e // 4, 4)) * 4 + lax.rem(yc + lax.rem(e, 4), 4)
        where = (gz + (e // 16) * (mirror - gz), other)
        pl.semaphore_signal(barrier, inc=1, device_id=where, device_id_type=MESH)
        return carry

    lax.fori_loop(1, 32, greet, 0)

    def rows_times_rhs(dz):
        rows = table_rows(dz)
        high, low = nt[0, rows, :], nt[1, rows, :]
        return dot_nt(high, rhs[0]) + dot_nt(high, rhs[1]) + dot_nt(low, rhs[0])

    load_cur.wait()

    def take(place, carry):
        plane = plane_at(place)
        rows = pl.ds(pl.multiple_of(place * 32, 32), 32)
        for part in range(2):
            high, low = split(cur[part, plane])
            rhs[0, rows, part * 512 : part * 512 + 512] = high
            rhs[1, rows, part * 512 : part * 512 + 512] = low
        return carry

    lax.fori_loop(0, 8, take, 0)

    def forward_rows(i):
        load_nt[i].wait()
        total = rows_times_rhs(order[i])
        zb = column(order[i])
        t1[0, pl.ds(zb * 4, 4)] = total[:, :128].reshape(4, 64, 128)
        t1[1, pl.ds(zb * 4, 4)] = total[:, 128:].reshape(4, 64, 128)

    def unit(k, by_side):
        along = way if by_side is side else -way
        return [(2, by_side), (along, 0), (along, 1), (0, by_side)][k]

    other_side = 1 - side

    def swap_copy(k):
        dz, half = unit(k, side)
        return pltpu.make_async_remote_copy(
            src_ref=t1.at[half, pl.ds(column(dz) * 4, 4)],
            dst_ref=met.at[k],
            send_sem=send1.at[k],
            recv_sem=recv1.at[k],
            device_id=(mirror, gy),
            device_id_type=MESH,
        )

    def subtract(k):
        dz, half = unit(k, other_side)
        diff[k] = (t1[half, pl.ds(column(dz) * 4, 4)] - met[k]) * sign

    def spread_copy(k, dy):
        dz, half = unit(k, other_side)
        yb = lax.rem(yc + dy, 4)
        target = gz if k == 3 else mirror
        return pltpu.make_async_remote_copy(
            src_ref=diff.at[k, yb],
            dst_ref=r1.at[half, gy],
            send_sem=send2.at[k * 4 + dy],
            recv_sem=recv2.at[k * 4 + dy],
            device_id=(target, column(dz) * 4 + yb),
            device_id_type=MESH,
        )

    def hand_copy(k):
        dz, half = unit(k, side)
        if k == 3:
            half = other_side
        rows = pl.ds(column(-dz) * 4, 4)
        return pltpu.make_async_remote_copy(
            src_ref=r1.at[half, rows],
            dst_ref=r1.at[half, rows],
            send_sem=send3.at[k],
            recv_sem=recv3.at[k],
            device_id=(mirror, gy),
            device_id_type=MESH,
        )

    def meet(k):
        swap_copy(k).wait_recv()
        subtract(k)

        def start(dy, carry):
            spread_copy(k, dy).start()
            return carry

        if k == 3:
            r1[other_side, gy] = diff[3, yc]
        lax.fori_loop(1 if k == 3 else 0, 4, start, 0)

    def hand(k):
        def wait(dy, carry):
            spread_copy(k, dy).wait_recv()
            return carry

        lax.fori_loop(1 if k == 3 else 0, 4, wait, 0)
        hand_copy(k).start()

    def gather(read, zb, row_of):
        for part in range(2):
            rows = pl.ds(part * 32, 32)
            for half in range(2):
                pieces = [read(half, zb * 4 + i, rows) for i in range(4)]
                for p, piece in enumerate(regroup(pieces)):
                    high, low = split(piece)
                    start = pl.ds(pl.multiple_of(row_of(half * 4 + p) * 32, 32), 32)
                    lhs[0, start, part * 128 : part * 128 + 128] = high
                    lhs[1, start, part * 128 : part * 128 + 128] = low

    def lhs_times(dz, columns):
        rows = table_rows(dz)
        both = dot_nn(lhs[...].reshape(512, 256), nn[0, rows, columns])
        return both[:256] + both[256:] + dot_nn(lhs[0], nn[1, rows, columns])

    def forward_from(dz, first):
        gather(lambda half, s, rows: r1[half, s, rows, :], column(dz), lambda place: place)

        def one(n, carry):
            columns = pl.ds(pl.multiple_of(n * 256, 256), 256)
            value = lhs_times(dz, columns)
            spectrum[:, columns] = value if first else spectrum[:, columns] + value
            return carry

        lax.fori_loop(0, 4, one, 0)

    forward_rows(0)
    pl.semaphore_wait(barrier, 31)
    swap_copy(0).start()
    load_nn.start()
    load_kern.start()
    forward_rows(1)
    swap_copy(1).start()
    forward_rows(2)
    forward_rows(3)
    swap_copy(2).start()
    meet(0)
    swap_copy(3).start()
    meet(1)
    hand(0)
    meet(2)
    hand(1)
    meet(3)
    hand(2)
    hand(3)
    load_nn.wait()
    forward_from(-way, True)
    hand_copy(0).wait_recv()
    forward_from(2, False)
    hand_copy(1).wait_recv()
    hand_copy(2).wait_recv()
    forward_from(way, False)
    hand_copy(3).wait_recv()
    forward_from(0, False)
    load_kern.wait()

    def product(n, carry):
        ky = pl.ds(pl.multiple_of(n * 256, 256), 256)
        ky_im = pl.ds(pl.multiple_of(512 + n * 256, 256), 256)
        re, im = spectrum[:, ky], spectrum[:, ky_im]
        kre = jnp.concatenate([kern[0, plane_at(p), :, ky] for p in range(8)], axis=0)
        kim = jnp.concatenate([kern[1, plane_at(p), :, ky] for p in range(8)], axis=0)
        high, low = split(re * kim + im * kre)
        rhs[0, :, ky] = high
        rhs[1, :, ky] = low
        high, low = split(re * kre - im * kim)
        rhs[0, :, ky_im] = high
        rhs[1, :, ky_im] = low
        return carry

    lax.fori_loop(0, 2, product, 0)

    def return_copy(e):
        other = column(e // 4) * 4 + lax.rem(yc + e, 4)
        return pltpu.make_async_remote_copy(
            src_ref=t2.at[other],
            dst_ref=r2.at[gy],
            send_sem=send4.at[e],
            recv_sem=recv4.at[e],
            device_id=(gz, other),
            device_id_type=MESH,
        )

    def up_or_down(dy):
        return 1 - 2 * (dy // 2)

    def first_leg(dy):
        yb = lax.rem(yc + dy, 4)
        return pltpu.make_async_remote_copy(
            src_ref=t2.at[column(2) * 4 + yb],
            dst_ref=relayed.at[dy],
            send_sem=send5.at[dy],
            recv_sem=recv5.at[dy],
            device_id=(gz, column(up_or_down(dy)) * 4 + yb),
            device_id_type=MESH,
        )

    def second_leg(dy):
        step = up_or_down(dy)
        origin = column(-step) * 4 + lax.rem(yc + 4 - dy, 4)
        return pltpu.make_async_remote_copy(
            src_ref=relayed.at[dy],
            dst_ref=r2.at[origin],
            send_sem=send4.at[8 + dy],
            recv_sem=recv4.at[8 + dy],
            device_id=(gz, column(step) * 4 + yc),
            device_id_type=MESH,
        )

    def inverse_rows(i, carry):
        dz = lax.rem(2 + 3 * i + 3 * (i * (i + 3) // 2 - 2 * i), 4)
        zb = column(dz)
        t2[pl.ds(zb * 4, 4)] = rows_times_rhs(dz).reshape(4, 64, 256)

        def start(dy, inner):
            e = dz * 4 + dy

            @pl.when((e > 0) & (dz != 2))
            def _():
                return_copy(e).start()

            @pl.when(dz == 2)
            def _():
                first_leg(dy).start()

            return inner

        return lax.fori_loop(0, 4, start, carry)

    lax.fori_loop(0, 4, inverse_rows, 0)
    r2[gy] = t2[gy]

    def relay(dy, carry):
        first_leg(dy).wait_recv()
        second_leg(dy).start()
        return carry

    lax.fori_loop(0, 4, relay, 0)

    def arrived(e, carry):
        return_copy(e).wait_recv()
        return carry

    def arrived_relayed(dy, carry):
        second_leg(dy).wait_recv()
        return carry

    factor = sign * scale

    def back_from(dz, first):
        def read(half, s, rows):
            return r2[s, rows, half * 128 : half * 128 + 128]

        gather(read, column(dz), plane_at)

        def one(n, carry):
            columns = pl.ds(pl.multiple_of(n * 256, 256), 256)
            x = pl.ds(pl.multiple_of(lax.rem(n, 2) * 256, 256), 256)
            value = (lhs_times(dz, columns) * factor).reshape(8, 32, 256)
            part = 1 - n // 2
            out[part, :, :, x] = value if first else out[part, :, :, x] + value
            return carry

        lax.fori_loop(0, 4, one, 0)

    lax.fori_loop(1, 4, arrived, 0)
    back_from(0, True)
    lax.fori_loop(4, 8, arrived, 0)
    back_from(-1, False)
    lax.fori_loop(12, 16, arrived, 0)
    back_from(1, False)
    lax.fori_loop(0, 4, arrived_relayed, 0)
    back_from(2, False)

    def sent(e, carry):
        return_copy(e).wait_send()
        return carry

    def sent_relayed(dy, carry):
        first_leg(dy).wait_send()
        second_leg(dy).wait_send()
        return carry

    lax.fori_loop(1, 8, sent, 0)
    lax.fori_loop(12, 16, sent, 0)
    lax.fori_loop(0, 4, sent_relayed, 0)
    for k in range(4):
        swap_copy(k).wait_send()
        hand_copy(k).wait_send()
        for dy in range(1 if k == 3 else 0, 4):
            spread_copy(k, dy).wait_send()


def local(current, kernel):
    members = lax.axis_size("gz")
    groups = lax.axis_size("gy")
    nt, nn = dft_tables(512, groups)
    hbm = pl.BlockSpec(memory_space=pltpu.HBM)
    table = pltpu.VMEM((2, 1024, 1024), BF16)
    operands = [
        pltpu.VMEM((2, 256, 1024), BF16),
        pltpu.VMEM((2, 256, 256), BF16),
        pltpu.VMEM((256, 1024), F32),
    ]
    block = pltpu.VMEM(current.shape, F32)
    halves = pltpu.VMEM((2, groups, 64, 128), F32)
    units = pltpu.VMEM((4, 4, 64, 128), F32)
    whole = pltpu.VMEM((groups, 64, 256), F32)
    dma = pltpu.SemaphoreType.DMA
    return pl.pallas_call(
        functools.partial(body, members, 1.0 / (512 * 512)),
        out_shape=jax.ShapeDtypeStruct(current.shape, F32),
        in_specs=[hbm] * 4,
        out_specs=pl.BlockSpec(memory_space=pltpu.VMEM),
        scratch_shapes=[block, block, table, table]
        + operands
        + [halves, units, units, halves, whole, whole]
        + [dma((7,)), dma((4,)), dma((4,)), dma((16,)), dma((16,))]
        + [dma((4,)), dma((4,)), dma((16,)), dma((16,))]
        + [pltpu.VMEM((4, 64, 256), F32), dma((4,)), dma((4,))],
        compiler_params=pltpu.CompilerParams(
            collective_id=0, has_side_effects=True, vmem_limit_bytes=52 * 1024 * 1024
        ),
    )(current, kernel, jnp.asarray(nt), jnp.asarray(nn))


def solution(mesh):
    spec = P(None, "gz", "gy", None)
    return jax.shard_map(
        local, mesh=mesh, in_specs=(spec, spec), out_specs=spec, check_vma=False
    )
```

```python
import functools

import jax
import jax.numpy as jnp
import ml_dtypes
import numpy as np
from jax import lax
from jax.experimental import pallas as pl
from jax.experimental.pallas import tpu as pltpu
from jax.sharding import PartitionSpec as P

MESH = pl.DeviceIdType.MESH
F32 = jnp.float32
BF16 = jnp.bfloat16


def two_terms(table):
    high = table.astype(ml_dtypes.bfloat16)
    low = (table - high.astype(np.float64)).astype(ml_dtypes.bfloat16)
    return np.stack([high, low])


def dft_tables(length, groups):
    index = np.arange(length)
    angle = (index[:, None] * index[None, :] % length) * (2.0 * np.pi / length)
    cos, sin = np.cos(angle), np.sin(angle)
    full = np.block([[cos, sin], [-sin, cos]])
    block = length // groups
    rows = full.reshape(2, groups, block, 2 * length).transpose(1, 0, 2, 3)
    rows = rows.reshape(2 * length, 2 * length)
    down = full.T.reshape(2, 4, length // 4, 2 * length).transpose(1, 0, 2, 3)
    return two_terms(rows), two_terms(down.reshape(2 * length, 2 * length))


def split(value):
    high = value.astype(BF16)
    return high, (value - high.astype(F32)).astype(BF16)


def dot_nt(a, b):
    return lax.dot_general(a, b, (((1,), (1,)), ((), ())), preferred_element_type=F32)


def dot_nn(a, b):
    return jnp.dot(a, b, preferred_element_type=F32)


def regroup(pieces):
    lane = lax.broadcasted_iota(jnp.int32, pieces[0].shape, 1)
    low = lane < 64
    even = lax.rem(lane // 32, 2) == 0
    v0, v1, v2, v3 = pieces

    def halves(a, b):
        return (
            jnp.where(low, a, pltpu.roll(b, 64, 1)),
            jnp.where(low, pltpu.roll(a, 64, 1), b),
        )

    def quarters(a, b):
        return (
            jnp.where(even, a, pltpu.roll(b, 32, 1)),
            jnp.where(even, pltpu.roll(a, 96, 1), b),
        )

    a0, a2 = halves(v0, v2)
    a1, a3 = halves(v1, v3)
    return quarters(a0, a1) + quarters(a2, a3)


def body(
    members,
    scale,
    cur_hbm,
    kern_hbm,
    nt_hbm,
    nn_hbm,
    out,
    cur,
    kern,
    nt,
    nn,
    rhs,
    lhs,
    spectrum,
    t1,
    met,
    diff,
    r1,
    t2,
    r2,
    load_sem,
    send1,
    recv1,
    send2,
    recv2,
    send3,
    recv3,
    send4,
    recv4,
    relayed,
    send5,
    recv5,
):
    gz = lax.axis_index("gz")
    gy = lax.axis_index("gy")
    mirror = members - 1 - gz
    zh = gy // 4
    yc = lax.rem(gy, 4)
    side = gz // (members // 2)
    way = 1 - 2 * side
    sign = way.astype(F32)

    def column(dz):
        return lax.rem(zh + dz + 8, 4)

    def plane_at(place):
        return place + side * (7 - 2 * place)

    def table_rows(dz):
        return pl.ds(pl.multiple_of(column(dz) * 256, 256), 256)

    order = (2, way, 0, -way)
    load_cur = pltpu.make_async_copy(cur_hbm, cur, load_sem.at[0])
    load_kern = pltpu.make_async_copy(kern_hbm, kern, load_sem.at[1])
    load_nn = pltpu.make_async_copy(nn_hbm, nn, load_sem.at[2])
    load_nt = [
        pltpu.make_async_copy(
            nt_hbm.at[:, table_rows(dz)], nt.at[:, table_rows(dz)], load_sem.at[3 + i]
        )
        for i, dz in enumerate(order)
    ]
    load_cur.start()
    for load in load_nt:
        load.start()

    barrier = pltpu.get_barrier_semaphore()

    def greet(e, carry):
        other = column(lax.rem(e // 4, 4)) * 4 + lax.rem(yc + lax.rem(e, 4), 4)
        where = (gz + (e // 16) * (mirror - gz), other)
        pl.semaphore_signal(barrier, inc=1, device_id=where, device_id_type=MESH)
        return carry

    lax.fori_loop(1, 32, greet, 0)

    def rows_times_rhs(dz):
        rows = table_rows(dz)
        high, low = nt[0, rows, :], nt[1, rows, :]
        return dot_nt(high, rhs[0]) + dot_nt(high, rhs[1]) + dot_nt(low, rhs[0])

    load_cur.wait()

    def take(place, carry):
        plane = plane_at(place)
        rows = pl.ds(pl.multiple_of(place * 32, 32), 32)
        for part in range(2):
            high, low = split(cur[part, plane])
            rhs[0, rows, part * 512 : part * 512 + 512] = high
            rhs[1, rows, part * 512 : part * 512 + 512] = low
        return carry

    lax.fori_loop(0, 8, take, 0)

    def forward_rows(i):
        load_nt[i].wait()
        total = rows_times_rhs(order[i])
        zb = column(order[i])
        t1[0, pl.ds(zb * 4, 4)] = total[:, :128].reshape(4, 64, 128)
        t1[1, pl.ds(zb * 4, 4)] = total[:, 128:].reshape(4, 64, 128)

    def unit(k, by_side):
        along = way if by_side is side else -way
        return [(2, by_side), (along, 0), (along, 1), (0, by_side)][k]

    other_side = 1 - side

    def swap_copy(k):
        dz, half = unit(k, side)
        return pltpu.make_async_remote_copy(
            src_ref=t1.at[half, pl.ds(column(dz) * 4, 4)],
            dst_ref=met.at[k],
            send_sem=send1.at[k],
            recv_sem=recv1.at[k],
            device_id=(mirror, gy),
            device_id_type=MESH,
        )

    def subtract(k):
        dz, half = unit(k, other_side)
        diff[k] = (t1[half, pl.ds(column(dz) * 4, 4)] - met[k]) * sign

    def spread_copy(k, dy):
        dz, half = unit(k, other_side)
        yb = lax.rem(yc + dy, 4)
        target = gz if k == 3 else mirror
        return pltpu.make_async_remote_copy(
            src_ref=diff.at[k, yb],
            dst_ref=r1.at[half, gy],
            send_sem=send2.at[k * 4 + dy],
            recv_sem=recv2.at[k * 4 + dy],
            device_id=(target, column(dz) * 4 + yb),
            device_id_type=MESH,
        )

    def hand_copy(k):
        dz, half = unit(k, side)
        if k == 3:
            half = other_side
        rows = pl.ds(column(-dz) * 4, 4)
        return pltpu.make_async_remote_copy(
            src_ref=r1.at[half, rows],
            dst_ref=r1.at[half, rows],
            send_sem=send3.at[k],
            recv_sem=recv3.at[k],
            device_id=(mirror, gy),
            device_id_type=MESH,
        )

    def meet(k):
        swap_copy(k).wait_recv()
        subtract(k)

        def start(dy, carry):
            spread_copy(k, dy).start()
            return carry

        if k == 3:
            r1[other_side, gy] = diff[3, yc]
        lax.fori_loop(1 if k == 3 else 0, 4, start, 0)

    def hand(k):
        def wait(dy, carry):
            spread_copy(k, dy).wait_recv()
            return carry

        lax.fori_loop(1 if k == 3 else 0, 4, wait, 0)
        hand_copy(k).start()

    def gather(read, zb, row_of):
        for part in range(2):
            rows = pl.ds(part * 32, 32)
            for half in range(2):
                pieces = [read(half, zb * 4 + i, rows) for i in range(4)]
                for p, piece in enumerate(regroup(pieces)):
                    high, low = split(piece)
                    start = pl.ds(pl.multiple_of(row_of(half * 4 + p) * 32, 32), 32)
                    lhs[0, start, part * 128 : part * 128 + 128] = high
                    lhs[1, start, part * 128 : part * 128 + 128] = low

    def lhs_times(dz, columns):
        rows = table_rows(dz)
        both = dot_nn(lhs[...].reshape(512, 256), nn[0, rows, columns])
        return both[:256] + both[256:] + dot_nn(lhs[0], nn[1, rows, columns])

    def forward_from(dz, first):
        gather(lambda half, s, rows: r1[half, s, rows, :], column(dz), lambda place: place)

        def one(n, carry):
            columns = pl.ds(pl.multiple_of(n * 256, 256), 256)
            value = lhs_times(dz, columns)
            spectrum[:, columns] = value if first else spectrum[:, columns] + value
            return carry

        lax.fori_loop(0, 4, one, 0)

    forward_rows(0)
    pl.semaphore_wait(barrier, 31)
    swap_copy(0).start()
    load_nn.start()
    load_kern.start()
    forward_rows(1)
    swap_copy(1).start()
    forward_rows(2)
    forward_rows(3)
    swap_copy(2).start()
    meet(0)
    swap_copy(3).start()
    meet(1)
    hand(0)
    meet(2)
    hand(1)
    meet(3)
    hand(2)
    hand(3)
    load_nn.wait()
    forward_from(-way, True)
    hand_copy(0).wait_recv()
    forward_from(2, False)
    hand_copy(1).wait_recv()
    hand_copy(2).wait_recv()
    forward_from(way, False)
    hand_copy(3).wait_recv()
    forward_from(0, False)
    load_kern.wait()

    def product(n, carry):
        ky = pl.ds(pl.multiple_of(n * 256, 256), 256)
        ky_im = pl.ds(pl.multiple_of(512 + n * 256, 256), 256)
        re, im = spectrum[:, ky], spectrum[:, ky_im]
        kre = jnp.concatenate([kern[0, plane_at(p), :, ky] for p in range(8)], axis=0)
        kim = jnp.concatenate([kern[1, plane_at(p), :, ky] for p in range(8)], axis=0)
        high, low = split(re * kim + im * kre)
        rhs[0, :, ky] = high
        rhs[1, :, ky] = low
        high, low = split(re * kre - im * kim)
        rhs[0, :, ky_im] = high
        rhs[1, :, ky_im] = low
        return carry

    lax.fori_loop(0, 2, product, 0)

    def return_copy(e):
        other = column(e // 4) * 4 + lax.rem(yc + e, 4)
        return pltpu.make_async_remote_copy(
            src_ref=t2.at[other],
            dst_ref=r2.at[gy],
            send_sem=send4.at[e],
            recv_sem=recv4.at[e],
            device_id=(gz, other),
            device_id_type=MESH,
        )

    def up_or_down(dy):
        return 1 - 2 * lax.rem(dy, 2)

    def first_leg(dy):
        yb = lax.rem(yc + dy, 4)
        return pltpu.make_async_remote_copy(
            src_ref=t2.at[column(2) * 4 + yb],
            dst_ref=relayed.at[dy],
            send_sem=send5.at[dy],
            recv_sem=recv5.at[dy],
            device_id=(gz, column(up_or_down(dy)) * 4 + yb),
            device_id_type=MESH,
        )

    def second_leg(dy):
        step = up_or_down(dy)
        origin = column(-step) * 4 + lax.rem(yc + 4 - dy, 4)
        return pltpu.make_async_remote_copy(
            src_ref=relayed.at[dy],
            dst_ref=r2.at[origin],
            send_sem=send4.at[8 + dy],
            recv_sem=recv4.at[8 + dy],
            device_id=(gz, column(step) * 4 + yc),
            device_id_type=MESH,
        )

    def inverse_rows(dz):
        t2[pl.ds(column(dz) * 4, 4)] = rows_times_rhs(dz).reshape(4, 64, 256)

    def start_far(dy, carry):
        first_leg(dy).start()
        return carry

    def start_near(dy, carry):
        return_copy(4 + dy).start()
        return_copy(12 + dy).start()
        return carry

    def start_own(dy, carry):
        return_copy(dy).start()
        return carry

    inverse_rows(2)
    lax.fori_loop(0, 4, start_far, 0)
    inverse_rows(1)
    inverse_rows(-1)
    lax.fori_loop(0, 4, start_near, 0)
    inverse_rows(0)
    lax.fori_loop(1, 4, start_own, 0)
    r2[gy] = t2[gy]

    def relay(dy, carry):
        first_leg(dy).wait_recv()
        second_leg(dy).start()
        return carry

    lax.fori_loop(0, 4, relay, 0)

    def arrived(e, carry):
        return_copy(e).wait_recv()
        return carry

    def arrived_relayed(dy, carry):
        second_leg(dy).wait_recv()
        return carry

    factor = sign * scale

    def back_from(dz, first):
        def read(half, s, rows):
            return r2[s, rows, half * 128 : half * 128 + 128]

        gather(read, column(dz), plane_at)

        def one(n, carry):
            columns = pl.ds(pl.multiple_of(n * 256, 256), 256)
            x = pl.ds(pl.multiple_of(lax.rem(n, 2) * 256, 256), 256)
            value = (lhs_times(dz, columns) * factor).reshape(8, 32, 256)
            part = 1 - n // 2
            out[part, :, :, x] = value if first else out[part, :, :, x] + value
            return carry

        lax.fori_loop(0, 4, one, 0)

    lax.fori_loop(1, 4, arrived, 0)
    back_from(0, True)
    lax.fori_loop(4, 8, arrived, 0)
    back_from(-1, False)
    lax.fori_loop(12, 16, arrived, 0)
    back_from(1, False)
    lax.fori_loop(0, 4, arrived_relayed, 0)
    back_from(2, False)

    def sent(e, carry):
        return_copy(e).wait_send()
        return carry

    def sent_relayed(dy, carry):
        first_leg(dy).wait_send()
        second_leg(dy).wait_send()
        return carry

    lax.fori_loop(1, 8, sent, 0)
    lax.fori_loop(12, 16, sent, 0)
    lax.fori_loop(0, 4, sent_relayed, 0)
    for k in range(4):
        swap_copy(k).wait_send()
        hand_copy(k).wait_send()
        for dy in range(1 if k == 3 else 0, 4):
            spread_copy(k, dy).wait_send()


def local(current, kernel):
    members = lax.axis_size("gz")
    groups = lax.axis_size("gy")
    nt, nn = dft_tables(512, groups)
    hbm = pl.BlockSpec(memory_space=pltpu.HBM)
    table = pltpu.VMEM((2, 1024, 1024), BF16)
    operands = [
        pltpu.VMEM((2, 256, 1024), BF16),
        pltpu.VMEM((2, 256, 256), BF16),
        pltpu.VMEM((256, 1024), F32),
    ]
    block = pltpu.VMEM(current.shape, F32)
    halves = pltpu.VMEM((2, groups, 64, 128), F32)
    units = pltpu.VMEM((4, 4, 64, 128), F32)
    whole = pltpu.VMEM((groups, 64, 256), F32)
    dma = pltpu.SemaphoreType.DMA
    return pl.pallas_call(
        functools.partial(body, members, 1.0 / (512 * 512)),
        out_shape=jax.ShapeDtypeStruct(current.shape, F32),
        in_specs=[hbm] * 4,
        out_specs=pl.BlockSpec(memory_space=pltpu.VMEM),
        scratch_shapes=[block, block, table, table]
        + operands
        + [halves, units, units, halves, whole, whole]
        + [dma((7,)), dma((4,)), dma((4,)), dma((16,)), dma((16,))]
        + [dma((4,)), dma((4,)), dma((16,)), dma((16,))]
        + [pltpu.VMEM((4, 64, 256), F32), dma((4,)), dma((4,))],
        compiler_params=pltpu.CompilerParams(
            collective_id=0, has_side_effects=True, vmem_limit_bytes=52 * 1024 * 1024
        ),
    )(current, kernel, jnp.asarray(nt), jnp.asarray(nn))


def solution(mesh):
    spec = P(None, "gz", "gy", None)
    return jax.shard_map(
        local, mesh=mesh, in_specs=(spec, spec), out_specs=spec, check_vma=False
    )
```

```python
import functools

import jax
import jax.numpy as jnp
import ml_dtypes
import numpy as np
from jax import lax
from jax.experimental import pallas as pl
from jax.experimental.pallas import tpu as pltpu
from jax.sharding import PartitionSpec as P

MESH = pl.DeviceIdType.MESH
F32 = jnp.float32
BF16 = jnp.bfloat16


def two_terms(table):
    high = table.astype(ml_dtypes.bfloat16)
    low = (table - high.astype(np.float64)).astype(ml_dtypes.bfloat16)
    return np.stack([high, low])


def dft_tables(length, groups):
    index = np.arange(length)
    angle = (index[:, None] * index[None, :] % length) * (2.0 * np.pi / length)
    cos, sin = np.cos(angle), np.sin(angle)
    full = np.block([[cos, sin], [-sin, cos]])
    block = length // groups
    rows = full.reshape(2, groups, block, 2 * length).transpose(1, 0, 2, 3)
    rows = rows.reshape(2 * length, 2 * length)
    down = full.T.reshape(2, 4, length // 4, 2 * length).transpose(1, 0, 2, 3)
    return two_terms(rows), two_terms(down.reshape(2 * length, 2 * length))


def split(value):
    high = value.astype(BF16)
    return high, (value - high.astype(F32)).astype(BF16)


def dot_nt(a, b):
    return lax.dot_general(a, b, (((1,), (1,)), ((), ())), preferred_element_type=F32)


def dot_nn(a, b):
    return jnp.dot(a, b, preferred_element_type=F32)


def regroup(pieces):
    lane = lax.broadcasted_iota(jnp.int32, pieces[0].shape, 1)
    low = lane < 64
    even = lax.rem(lane // 32, 2) == 0
    v0, v1, v2, v3 = pieces

    def halves(a, b):
        return (
            jnp.where(low, a, pltpu.roll(b, 64, 1)),
            jnp.where(low, pltpu.roll(a, 64, 1), b),
        )

    def quarters(a, b):
        return (
            jnp.where(even, a, pltpu.roll(b, 32, 1)),
            jnp.where(even, pltpu.roll(a, 96, 1), b),
        )

    a0, a2 = halves(v0, v2)
    a1, a3 = halves(v1, v3)
    return quarters(a0, a1) + quarters(a2, a3)


def body(
    members,
    scale,
    cur_hbm,
    kern_hbm,
    nt_hbm,
    nn_hbm,
    out,
    cur,
    kern,
    nt,
    nn,
    rhs,
    lhs,
    spectrum,
    t1,
    met,
    diff,
    r1,
    t2,
    r2,
    load_sem,
    send1,
    recv1,
    send2,
    recv2,
    send3,
    recv3,
    send4,
    recv4,
    relayed,
    send5,
    recv5,
):
    gz = lax.axis_index("gz")
    gy = lax.axis_index("gy")
    mirror = members - 1 - gz
    zh = gy // 4
    yc = lax.rem(gy, 4)
    side = gz // (members // 2)
    way = 1 - 2 * side
    sign = way.astype(F32)

    def column(dz):
        return lax.rem(zh + dz + 8, 4)

    def plane_at(place):
        return place + side * (7 - 2 * place)

    def table_rows(dz):
        return pl.ds(pl.multiple_of(column(dz) * 256, 256), 256)

    order = (2, way, 0, -way)
    load_cur = pltpu.make_async_copy(cur_hbm, cur, load_sem.at[0])
    load_kern = pltpu.make_async_copy(kern_hbm, kern, load_sem.at[1])
    load_nn = pltpu.make_async_copy(nn_hbm, nn, load_sem.at[2])
    load_nt = [
        pltpu.make_async_copy(
            nt_hbm.at[:, table_rows(dz)], nt.at[:, table_rows(dz)], load_sem.at[3 + i]
        )
        for i, dz in enumerate(order)
    ]
    load_cur.start()
    for load in load_nt:
        load.start()

    barrier = pltpu.get_barrier_semaphore()

    def greet(e, carry):
        other = column(lax.rem(e // 4, 4)) * 4 + lax.rem(yc + lax.rem(e, 4), 4)
        where = (gz + (e // 16) * (mirror - gz), other)
        pl.semaphore_signal(barrier, inc=1, device_id=where, device_id_type=MESH)
        return carry

    lax.fori_loop(1, 32, greet, 0)

    def rows_times_rhs(dz):
        rows = table_rows(dz)
        high, low = nt[0, rows, :], nt[1, rows, :]
        return dot_nt(high, rhs[0]) + dot_nt(high, rhs[1]) + dot_nt(low, rhs[0])

    load_cur.wait()

    def take(place, carry):
        plane = plane_at(place)
        rows = pl.ds(pl.multiple_of(place * 32, 32), 32)
        for part in range(2):
            high, low = split(cur[part, plane])
            rhs[0, rows, part * 512 : part * 512 + 512] = high
            rhs[1, rows, part * 512 : part * 512 + 512] = low
        return carry

    lax.fori_loop(0, 8, take, 0)

    def forward_rows(i):
        load_nt[i].wait()
        total = rows_times_rhs(order[i])
        zb = column(order[i])
        t1[0, pl.ds(zb * 4, 4)] = total[:, :128].reshape(4, 64, 128)
        t1[1, pl.ds(zb * 4, 4)] = total[:, 128:].reshape(4, 64, 128)

    def unit(k, by_side):
        along = way if by_side is side else -way
        return [(2, by_side), (along, 0), (along, 1), (0, by_side)][k]

    inner = lax.rem((gz * 4 // members + 1) // 2, 2)

    other_side = 1 - side

    def swap_copy(k):
        dz, half = unit(k, side)
        return pltpu.make_async_remote_copy(
            src_ref=t1.at[half, pl.ds(column(dz) * 4, 4)],
            dst_ref=met.at[k],
            send_sem=send1.at[k],
            recv_sem=recv1.at[k],
            device_id=(mirror, gy),
            device_id_type=MESH,
        )

    def subtract(k):
        dz, half = unit(k, other_side)
        diff[k] = (t1[half, pl.ds(column(dz) * 4, 4)] - met[k]) * sign

    def spread_copy(k, dy):
        dz, half = unit(k, other_side)
        yb = lax.rem(yc + dy, 4)
        target = gz if k == 3 else mirror
        return pltpu.make_async_remote_copy(
            src_ref=diff.at[k, yb],
            dst_ref=r1.at[half, gy],
            send_sem=send2.at[k * 4 + dy],
            recv_sem=recv2.at[k * 4 + dy],
            device_id=(target, column(dz) * 4 + yb),
            device_id_type=MESH,
        )

    def hand_copy(k):
        dz, half = unit(k, side)
        if k == 3:
            half = other_side
        rows = pl.ds(column(-dz) * 4, 4)
        return pltpu.make_async_remote_copy(
            src_ref=r1.at[half, rows],
            dst_ref=r1.at[half, rows],
            send_sem=send3.at[k],
            recv_sem=recv3.at[k],
            device_id=(mirror, gy),
            device_id_type=MESH,
        )

    def meet(k):
        swap_copy(k).wait_recv()
        subtract(k)

        def start(dy, carry):
            spread_copy(k, dy).start()
            return carry

        if k == 3:
            r1[other_side, gy] = diff[3, yc]
        lax.fori_loop(1 if k == 3 else 0, 4, start, 0)

    def hand(k):
        def wait(dy, carry):
            spread_copy(k, dy).wait_recv()
            return carry

        lax.fori_loop(1 if k == 3 else 0, 4, wait, 0)
        hand_copy(k).start()

    def gather(read, zb, row_of):
        for part in range(2):
            rows = pl.ds(part * 32, 32)
            for half in range(2):
                pieces = [read(half, zb * 4 + i, rows) for i in range(4)]
                for p, piece in enumerate(regroup(pieces)):
                    high, low = split(piece)
                    start = pl.ds(pl.multiple_of(row_of(half * 4 + p) * 32, 32), 32)
                    lhs[0, start, part * 128 : part * 128 + 128] = high
                    lhs[1, start, part * 128 : part * 128 + 128] = low

    def lhs_times(dz, columns):
        rows = table_rows(dz)
        both = dot_nn(lhs[...].reshape(512, 256), nn[0, rows, columns])
        return both[:256] + both[256:] + dot_nn(lhs[0], nn[1, rows, columns])

    def forward_from(dz, first):
        gather(lambda half, s, rows: r1[half, s, rows, :], column(dz), lambda place: place)

        def one(n, carry):
            columns = pl.ds(pl.multiple_of(n * 256, 256), 256)
            value = lhs_times(dz, columns)
            spectrum[:, columns] = value if first else spectrum[:, columns] + value
            return carry

        lax.fori_loop(0, 4, one, 0)

    forward_rows(0)
    pl.semaphore_wait(barrier, 31)
    swap_copy(0).start()
    load_nn.start()
    load_kern.start()
    forward_rows(1)
    swap_copy(1).start()
    forward_rows(2)
    forward_rows(3)
    swap_copy(2).start()
    meet(0)
    swap_copy(3).start()
    meet(1)
    hand(0)
    meet(2)
    hand(1)
    meet(3)
    hand(2)
    hand(3)
    load_nn.wait()
    forward_from(-way, True)
    hand_copy(0).wait_recv()
    forward_from(2, False)
    hand_copy(1).wait_recv()
    hand_copy(2).wait_recv()
    forward_from(way, False)
    hand_copy(3).wait_recv()
    forward_from(0, False)
    load_kern.wait()

    def product(n, carry):
        ky = pl.ds(pl.multiple_of(n * 256, 256), 256)
        ky_im = pl.ds(pl.multiple_of(512 + n * 256, 256), 256)
        re, im = spectrum[:, ky], spectrum[:, ky_im]
        kre = jnp.concatenate([kern[0, plane_at(p), :, ky] for p in range(8)], axis=0)
        kim = jnp.concatenate([kern[1, plane_at(p), :, ky] for p in range(8)], axis=0)
        high, low = split(re * kim + im * kre)
        rhs[0, :, ky] = high
        rhs[1, :, ky] = low
        high, low = split(re * kre - im * kim)
        rhs[0, :, ky_im] = high
        rhs[1, :, ky_im] = low
        return carry

    lax.fori_loop(0, 2, product, 0)

    def return_copy(e):
        other = column(e // 4) * 4 + lax.rem(yc + e, 4)
        return pltpu.make_async_remote_copy(
            src_ref=t2.at[other],
            dst_ref=r2.at[gy],
            send_sem=send4.at[e],
            recv_sem=recv4.at[e],
            device_id=(gz, other),
            device_id_type=MESH,
        )

    def up_or_down(dy):
        return 1 - 2 * lax.rem(dy, 2)

    def first_leg(dy):
        yb = lax.rem(yc + dy, 4)
        return pltpu.make_async_remote_copy(
            src_ref=t2.at[column(2) * 4 + yb],
            dst_ref=relayed.at[dy],
            send_sem=send5.at[dy],
            recv_sem=recv5.at[dy],
            device_id=(gz, column(up_or_down(dy)) * 4 + yb),
            device_id_type=MESH,
        )

    def second_leg(dy):
        step = up_or_down(dy)
        origin = column(-step) * 4 + lax.rem(yc + 4 - dy, 4)
        return pltpu.make_async_remote_copy(
            src_ref=relayed.at[dy],
            dst_ref=r2.at[origin],
            send_sem=send4.at[8 + dy],
            recv_sem=recv4.at[8 + dy],
            device_id=(gz, column(step) * 4 + yc),
            device_id_type=MESH,
        )

    def inverse_rows(dz):
        t2[pl.ds(column(dz) * 4, 4)] = rows_times_rhs(dz).reshape(4, 64, 256)

    def start_far(dy, carry):
        first_leg(dy).start()
        return carry

    def start_near(dy, carry):
        return_copy(4 + dy).start()
        return_copy(12 + dy).start()

        @pl.when(inner == 0)
        def _():
            return_copy(4 + dy).wait_send()
            return_copy(12 + dy).wait_send()

        return carry

    def start_own(dy, carry):
        return_copy(dy).start()
        return carry

    inverse_rows(2)
    lax.fori_loop(0, 4, start_far, 0)
    inverse_rows(1)
    inverse_rows(-1)
    lax.fori_loop(0, 4, start_near, 0)
    inverse_rows(0)
    lax.fori_loop(1, 4, start_own, 0)
    r2[gy] = t2[gy]

    def relay(dy, carry):
        first_leg(dy).wait_recv()
        second_leg(dy).start()
        return carry

    lax.fori_loop(0, 4, relay, 0)

    def arrived(e, carry):
        return_copy(e).wait_recv()
        return carry

    def arrived_relayed(dy, carry):
        second_leg(dy).wait_recv()
        return carry

    factor = sign * scale

    def back_from(dz, first):
        def read(half, s, rows):
            return r2[s, rows, half * 128 : half * 128 + 128]

        gather(read, column(dz), plane_at)

        def one(n, carry):
            columns = pl.ds(pl.multiple_of(n * 256, 256), 256)
            x = pl.ds(pl.multiple_of(lax.rem(n, 2) * 256, 256), 256)
            value = (lhs_times(dz, columns) * factor).reshape(8, 32, 256)
            part = 1 - n // 2
            out[part, :, :, x] = value if first else out[part, :, :, x] + value
            return carry

        lax.fori_loop(0, 4, one, 0)

    lax.fori_loop(1, 4, arrived, 0)
    back_from(0, True)
    lax.fori_loop(4, 8, arrived, 0)
    back_from(-1, False)
    lax.fori_loop(12, 16, arrived, 0)
    back_from(1, False)
    lax.fori_loop(0, 4, arrived_relayed, 0)
    back_from(2, False)

    def sent(e, carry):
        return_copy(e).wait_send()
        return carry

    def sent_relayed(dy, carry):
        first_leg(dy).wait_send()
        second_leg(dy).wait_send()
        return carry

    lax.fori_loop(1, 4, sent, 0)

    @pl.when(inner == 1)
    def _():
        lax.fori_loop(4, 8, sent, 0)
        lax.fori_loop(12, 16, sent, 0)

    lax.fori_loop(0, 4, sent_relayed, 0)
    for k in range(4):
        swap_copy(k).wait_send()
        hand_copy(k).wait_send()
        for dy in range(1 if k == 3 else 0, 4):
            spread_copy(k, dy).wait_send()


def local(current, kernel):
    members = lax.axis_size("gz")
    groups = lax.axis_size("gy")
    nt, nn = dft_tables(512, groups)
    hbm = pl.BlockSpec(memory_space=pltpu.HBM)
    table = pltpu.VMEM((2, 1024, 1024), BF16)
    operands = [
        pltpu.VMEM((2, 256, 1024), BF16),
        pltpu.VMEM((2, 256, 256), BF16),
        pltpu.VMEM((256, 1024), F32),
    ]
    block = pltpu.VMEM(current.shape, F32)
    halves = pltpu.VMEM((2, groups, 64, 128), F32)
    units = pltpu.VMEM((4, 4, 64, 128), F32)
    whole = pltpu.VMEM((groups, 64, 256), F32)
    dma = pltpu.SemaphoreType.DMA
    return pl.pallas_call(
        functools.partial(body, members, 1.0 / (512 * 512)),
        out_shape=jax.ShapeDtypeStruct(current.shape, F32),
        in_specs=[hbm] * 4,
        out_specs=pl.BlockSpec(memory_space=pltpu.VMEM),
        scratch_shapes=[block, block, table, table]
        + operands
        + [halves, units, units, halves, whole, whole]
        + [dma((7,)), dma((4,)), dma((4,)), dma((16,)), dma((16,))]
        + [dma((4,)), dma((4,)), dma((16,)), dma((16,))]
        + [pltpu.VMEM((4, 64, 256), F32), dma((4,)), dma((4,))],
        compiler_params=pltpu.CompilerParams(
            collective_id=0, has_side_effects=True, vmem_limit_bytes=52 * 1024 * 1024
        ),
    )(current, kernel, jnp.asarray(nt), jnp.asarray(nn))


def solution(mesh):
    spec = P(None, "gz", "gy", None)
    return jax.shard_map(
        local, mesh=mesh, in_specs=(spec, spec), out_specs=spec, check_vma=False
    )
```

```python
import functools

import jax
import jax.numpy as jnp
import ml_dtypes
import numpy as np
from jax import lax
from jax.experimental import pallas as pl
from jax.experimental.pallas import tpu as pltpu
from jax.sharding import PartitionSpec as P

MESH = pl.DeviceIdType.MESH
F32 = jnp.float32
BF16 = jnp.bfloat16


def two_terms(table):
    high = table.astype(ml_dtypes.bfloat16)
    low = (table - high.astype(np.float64)).astype(ml_dtypes.bfloat16)
    return np.stack([high, low])


def dft_tables(length, groups):
    index = np.arange(length)
    angle = (index[:, None] * index[None, :] % length) * (2.0 * np.pi / length)
    cos, sin = np.cos(angle), np.sin(angle)
    full = np.block([[cos, sin], [-sin, cos]])
    block = length // groups
    rows = full.reshape(2, groups, block, 2 * length).transpose(1, 0, 2, 3)
    rows = rows.reshape(2 * length, 2 * length)
    down = full.T.reshape(2, 4, length // 4, 2 * length).transpose(1, 0, 2, 3)
    return two_terms(rows), two_terms(down.reshape(2 * length, 2 * length))


def split(value):
    high = value.astype(BF16)
    return high, (value - high.astype(F32)).astype(BF16)


def dot_nt(a, b):
    return lax.dot_general(a, b, (((1,), (1,)), ((), ())), preferred_element_type=F32)


def dot_nn(a, b):
    return jnp.dot(a, b, preferred_element_type=F32)


def regroup(pieces):
    lane = lax.broadcasted_iota(jnp.int32, pieces[0].shape, 1)
    low = lane < 64
    even = lax.rem(lane // 32, 2) == 0
    v0, v1, v2, v3 = pieces

    def halves(a, b):
        return (
            jnp.where(low, a, pltpu.roll(b, 64, 1)),
            jnp.where(low, pltpu.roll(a, 64, 1), b),
        )

    def quarters(a, b):
        return (
            jnp.where(even, a, pltpu.roll(b, 32, 1)),
            jnp.where(even, pltpu.roll(a, 96, 1), b),
        )

    a0, a2 = halves(v0, v2)
    a1, a3 = halves(v1, v3)
    return quarters(a0, a1) + quarters(a2, a3)


def body(
    members,
    scale,
    cur_hbm,
    kern_hbm,
    nt_hbm,
    nn_hbm,
    out,
    cur,
    kern,
    nt,
    nn,
    rhs,
    lhs,
    spectrum,
    t1,
    met,
    diff,
    r1,
    t2,
    r2,
    load_sem,
    send1,
    recv1,
    send2,
    recv2,
    send3,
    recv3,
    send4,
    recv4,
):
    gz = lax.axis_index("gz")
    gy = lax.axis_index("gy")
    mirror = members - 1 - gz
    zh = gy // 4
    yc = lax.rem(gy, 4)
    side = gz // (members // 2)
    way = 1 - 2 * side
    sign = way.astype(F32)

    def column(dz):
        return lax.rem(zh + dz + 8, 4)

    def plane_at(place):
        return place + side * (7 - 2 * place)

    def table_rows(dz):
        return pl.ds(pl.multiple_of(column(dz) * 256, 256), 256)

    order = (2, way, 0, -way)
    load_cur = pltpu.make_async_copy(cur_hbm, cur, load_sem.at[0])
    load_kern = pltpu.make_async_copy(kern_hbm, kern, load_sem.at[1])
    load_nn = pltpu.make_async_copy(nn_hbm, nn, load_sem.at[2])
    load_nt = [
        pltpu.make_async_copy(
            nt_hbm.at[:, table_rows(dz)], nt.at[:, table_rows(dz)], load_sem.at[3 + i]
        )
        for i, dz in enumerate(order)
    ]
    load_cur.start()
    for load in load_nt:
        load.start()

    barrier = pltpu.get_barrier_semaphore()

    def greet(e, carry):
        other = column(lax.rem(e // 4, 4)) * 4 + lax.rem(yc + lax.rem(e, 4), 4)
        where = (gz + (e // 16) * (mirror - gz), other)
        pl.semaphore_signal(barrier, inc=1, device_id=where, device_id_type=MESH)
        return carry

    lax.fori_loop(1, 32, greet, 0)

    def rows_times_rhs(dz):
        rows = table_rows(dz)
        high, low = nt[0, rows, :], nt[1, rows, :]
        return dot_nt(high, rhs[0]) + dot_nt(high, rhs[1]) + dot_nt(low, rhs[0])

    load_cur.wait()

    def take(place, carry):
        plane = plane_at(place)
        rows = pl.ds(pl.multiple_of(place * 32, 32), 32)
        for part in range(2):
            high, low = split(cur[part, plane])
            rhs[0, rows, part * 512 : part * 512 + 512] = high
            rhs[1, rows, part * 512 : part * 512 + 512] = low
        return carry

    lax.fori_loop(0, 8, take, 0)

    def forward_rows(i):
        load_nt[i].wait()
        total = rows_times_rhs(order[i])
        zb = column(order[i])
        t1[0, pl.ds(zb * 4, 4)] = total[:, :128].reshape(4, 64, 128)
        t1[1, pl.ds(zb * 4, 4)] = total[:, 128:].reshape(4, 64, 128)

    def unit(k, by_side):
        along = way if by_side is side else -way
        return [(2, by_side), (along, 0), (along, 1), (0, by_side)][k]

    other_side = 1 - side

    def swap_copy(k):
        dz, half = unit(k, side)
        return pltpu.make_async_remote_copy(
            src_ref=t1.at[half, pl.ds(column(dz) * 4, 4)],
            dst_ref=met.at[k],
            send_sem=send1.at[k],
            recv_sem=recv1.at[k],
            device_id=(mirror, gy),
            device_id_type=MESH,
        )

    def subtract(k):
        dz, half = unit(k, other_side)
        diff[k] = (t1[half, pl.ds(column(dz) * 4, 4)] - met[k]) * sign

    def spread_copy(k, dy):
        dz, half = unit(k, other_side)
        yb = lax.rem(yc + dy, 4)
        target = gz if k == 3 else mirror
        return pltpu.make_async_remote_copy(
            src_ref=diff.at[k, yb],
            dst_ref=r1.at[half, gy],
            send_sem=send2.at[k * 4 + dy],
            recv_sem=recv2.at[k * 4 + dy],
            device_id=(target, column(dz) * 4 + yb),
            device_id_type=MESH,
        )

    def hand_copy(k):
        dz, half = unit(k, side)
        if k == 3:
            half = other_side
        rows = pl.ds(column(-dz) * 4, 4)
        return pltpu.make_async_remote_copy(
            src_ref=r1.at[half, rows],
            dst_ref=r1.at[half, rows],
            send_sem=send3.at[k],
            recv_sem=recv3.at[k],
            device_id=(mirror, gy),
            device_id_type=MESH,
        )

    def meet(k):
        swap_copy(k).wait_recv()
        subtract(k)

        def start(dy, carry):
            spread_copy(k, dy).start()
            return carry

        if k == 3:
            r1[other_side, gy] = diff[3, yc]
        lax.fori_loop(1 if k == 3 else 0, 4, start, 0)

    def hand(k):
        def wait(dy, carry):
            spread_copy(k, dy).wait_recv()
            return carry

        lax.fori_loop(1 if k == 3 else 0, 4, wait, 0)
        hand_copy(k).start()

    def gather(read, zb, row_of):
        for part in range(2):
            rows = pl.ds(part * 32, 32)
            for half in range(2):
                pieces = [read(half, zb * 4 + i, rows) for i in range(4)]
                for p, piece in enumerate(regroup(pieces)):
                    high, low = split(piece)
                    start = pl.ds(pl.multiple_of(row_of(half * 4 + p) * 32, 32), 32)
                    lhs[0, start, part * 128 : part * 128 + 128] = high
                    lhs[1, start, part * 128 : part * 128 + 128] = low

    def lhs_times(dz, columns):
        rows = table_rows(dz)
        both = dot_nn(lhs[...].reshape(512, 256), nn[0, rows, columns])
        return both[:256] + both[256:] + dot_nn(lhs[0], nn[1, rows, columns])

    def forward_from(dz, first):
        gather(lambda half, s, rows: r1[half, s, rows, :], column(dz), lambda place: place)

        def one(n, carry):
            columns = pl.ds(pl.multiple_of(n * 256, 256), 256)
            value = lhs_times(dz, columns)
            spectrum[:, columns] = value if first else spectrum[:, columns] + value
            return carry

        lax.fori_loop(0, 4, one, 0)

    forward_rows(0)
    pl.semaphore_wait(barrier, 31)
    swap_copy(0).start()
    load_nn.start()
    load_kern.start()
    forward_rows(1)
    swap_copy(1).start()
    forward_rows(2)
    forward_rows(3)
    swap_copy(2).start()
    meet(0)
    swap_copy(3).start()
    meet(1)
    hand(0)
    meet(2)
    hand(1)
    meet(3)
    hand(2)
    hand(3)
    load_nn.wait()
    forward_from(-way, True)
    hand_copy(0).wait_recv()
    forward_from(2, False)
    hand_copy(1).wait_recv()
    hand_copy(2).wait_recv()
    forward_from(way, False)
    hand_copy(3).wait_recv()
    forward_from(0, False)
    load_kern.wait()

    def product(n, carry):
        ky = pl.ds(pl.multiple_of(n * 256, 256), 256)
        ky_im = pl.ds(pl.multiple_of(512 + n * 256, 256), 256)
        re, im = spectrum[:, ky], spectrum[:, ky_im]
        kre = jnp.concatenate([kern[0, plane_at(p), :, ky] for p in range(8)], axis=0)
        kim = jnp.concatenate([kern[1, plane_at(p), :, ky] for p in range(8)], axis=0)
        high, low = split(re * kim + im * kre)
        rhs[0, :, ky] = high
        rhs[1, :, ky] = low
        high, low = split(re * kre - im * kim)
        rhs[0, :, ky_im] = high
        rhs[1, :, ky_im] = low
        return carry

    lax.fori_loop(0, 2, product, 0)

    def return_copy(e):
        other = column(e // 4) * 4 + lax.rem(yc + e, 4)
        return pltpu.make_async_remote_copy(
            src_ref=t2.at[other],
            dst_ref=r2.at[gy],
            send_sem=send4.at[e],
            recv_sem=recv4.at[e],
            device_id=(gz, other),
            device_id_type=MESH,
        )

    def inverse_rows(dz):
        t2[pl.ds(column(dz) * 4, 4)] = rows_times_rhs(dz).reshape(4, 64, 256)

    def start_far(dy, carry):
        return_copy(8 + dy).start()
        return carry

    def start_near(dy, carry):
        return_copy(4 + dy).start()
        return_copy(12 + dy).start()
        return carry

    def start_own(dy, carry):
        return_copy(dy).start()
        return carry

    inverse_rows(2)
    lax.fori_loop(0, 4, start_far, 0)
    inverse_rows(1)
    inverse_rows(-1)
    lax.fori_loop(0, 4, start_near, 0)
    inverse_rows(0)
    lax.fori_loop(1, 4, start_own, 0)
    r2[gy] = t2[gy]

    def arrived(e, carry):
        return_copy(e).wait_recv()
        return carry

    factor = sign * scale

    def back_from(dz, first):
        def read(half, s, rows):
            return r2[s, rows, half * 128 : half * 128 + 128]

        gather(read, column(dz), plane_at)

        def one(n, carry):
            columns = pl.ds(pl.multiple_of(n * 256, 256), 256)
            x = pl.ds(pl.multiple_of(lax.rem(n, 2) * 256, 256), 256)
            value = (lhs_times(dz, columns) * factor).reshape(8, 32, 256)
            part = 1 - n // 2
            out[part, :, :, x] = value if first else out[part, :, :, x] + value
            return carry

        lax.fori_loop(0, 4, one, 0)

    lax.fori_loop(1, 4, arrived, 0)
    back_from(0, True)
    lax.fori_loop(4, 8, arrived, 0)
    back_from(-1, False)
    lax.fori_loop(12, 16, arrived, 0)
    back_from(1, False)
    lax.fori_loop(8, 12, arrived, 0)
    back_from(2, False)

    def sent(e, carry):
        return_copy(e).wait_send()
        return carry

    lax.fori_loop(1, 16, sent, 0)
    for k in range(4):
        swap_copy(k).wait_send()
        hand_copy(k).wait_send()
        for dy in range(1 if k == 3 else 0, 4):
            spread_copy(k, dy).wait_send()


def local(current, kernel):
    members = lax.axis_size("gz")
    groups = lax.axis_size("gy")
    nt, nn = dft_tables(512, groups)
    hbm = pl.BlockSpec(memory_space=pltpu.HBM)
    table = pltpu.VMEM((2, 1024, 1024), BF16)
    operands = [
        pltpu.VMEM((2, 256, 1024), BF16),
        pltpu.VMEM((2, 256, 256), BF16),
        pltpu.VMEM((256, 1024), F32),
    ]
    block = pltpu.VMEM(current.shape, F32)
    halves = pltpu.VMEM((2, groups, 64, 128), F32)
    units = pltpu.VMEM((4, 4, 64, 128), F32)
    whole = pltpu.VMEM((groups, 64, 256), F32)
    dma = pltpu.SemaphoreType.DMA
    return pl.pallas_call(
        functools.partial(body, members, 1.0 / (512 * 512)),
        out_shape=jax.ShapeDtypeStruct(current.shape, F32),
        in_specs=[hbm] * 4,
        out_specs=pl.BlockSpec(memory_space=pltpu.VMEM),
        scratch_shapes=[block, block, table, table]
        + operands
        + [halves, units, units, halves, whole, whole]
        + [dma((7,)), dma((4,)), dma((4,)), dma((16,)), dma((16,))]
        + [dma((4,)), dma((4,)), dma((16,)), dma((16,))]
        + [],
        compiler_params=pltpu.CompilerParams(
            collective_id=0, has_side_effects=True, vmem_limit_bytes=52 * 1024 * 1024
        ),
    )(current, kernel, jnp.asarray(nt), jnp.asarray(nn))


def solution(mesh):
    spec = P(None, "gz", "gy", None)
    return jax.shard_map(
        local, mesh=mesh, in_specs=(spec, spec), out_specs=spec, check_vma=False
    )
```
